256 devices in a mesh: tel: 8 (over y, core), leaf: 32 (over z, x).
Axes of the slice: x: 4, y: 4, z: 8, core: 2. Of those that a mesh axis runs over, the one named last changes fastest.
Arguments:
- values: bfloat16 [32, 256, 8, 256], P('leaf', 'tel'), may hold values from -6 to 6
- basis: bfloat16 [32, 256, 64, 256], P('leaf', 'tel'), may hold values from -0.375 to 0.375
- transfer_b: bfloat16 [32, 32, 64, 512], P('leaf', 'tel'), may hold values from -0.5 to 0.5
- transfer_c: bfloat16 [32, 4, 64, 512], P('leaf'), may hold values from -0.5 to 0.5
- coupling_a: bfloat16 [32, 256, 24, 4096], P('leaf', 'tel'), may hold values from -0.21875 to 0.21875
- lists_a: int32 [32, 256, 24], P('leaf', 'tel'), may hold values from 0 to 8191, as said below
- mask_a: int32 [32, 256, 24], P('leaf', 'tel'), may hold values from 0 to 1, as said below
- coupling_b: bfloat16 [32, 32, 24, 4096], P('leaf', 'tel'), may hold values from -0.21875 to 0.21875
- lists_b: int32 [32, 32, 24], P('leaf', 'tel'), may hold values from 0 to 1023, as said below
- mask_b: int32 [32, 32, 24], P('leaf', 'tel'), may hold values from 0 to 1, as said below
- coupling_c: bfloat16 [32, 4, 24, 4096], P('leaf', None, 'tel'), may hold values from -0.21875 to 0.21875
- lists_c: int32 [32, 4, 24], P('leaf', None, 'tel'), may hold values from 0 to 127, as said below
- mask_c: int32 [32, 4, 24], P('leaf', None, 'tel'), may hold values from 0 to 1, as said below
Outputs:
- field: bfloat16 [32, 256, 8, 256], P('leaf', 'tel')
The draws below stay inside these ranges and needn't reach their ends.
Inputs may be any that keep to these rules, and one draw needn't show every extreme that they name: `lists_a`: the partner of a leaf in group g is a leaf of group g - 1, g or g + 1; both ends of the range occur. `lists_b`: the partner of a parent box in group g is a parent box of group g - 1, g or g + 1; both ends of the range occur. `lists_c`: partners of grandparent boxes may be any grandparent box; both ends of the range occur. `mask_a`: every list row has between a quarter of its entries and all of them valid, in any positions. `mask_b`: as for mask_a. `mask_c`: as for mask_a, counted over the whole row of 24 entries.
All inputs are finite; a program needn't handle non-finite values.
Results may differ from the reference program's by a relative error of at most 0.015.
Values may be sent and summed in bfloat16 or wider, within the bound.
A program may use at most 128 MiB of HBM per device.

```python
import jax
import jax.numpy as jnp
from jax import lax

RANK = 64
PTS = 256
RHS = 8
P_A = 24
P_B = 24
P_C = 24
GROUPS = 32
GLEAVES = 256
GB = 32
CPG = 4


def near_ids(key, groups, boxes, slots):
    first, second = jax.random.split(key)
    shape = (groups, boxes, slots)
    offset = jax.random.randint(first, shape, 0, 3) - 1
    owner = jnp.clip(jnp.arange(groups, dtype=jnp.int32)[:, None, None] + offset, 0, groups - 1)
    inner = jax.random.randint(second, shape, 0, boxes)
    ids = owner * boxes + inner
    ids = ids.at[0, 0, 0].set(0)
    return ids.at[groups - 1, boxes - 1, slots - 1].set(groups * boxes - 1).astype(jnp.int32)


def any_ids(key, groups, boxes, slots):
    ids = jax.random.randint(key, (groups, boxes, slots), 0, groups * boxes)
    ids = ids.at[0, 0, 0].set(0)
    return ids.at[groups - 1, boxes - 1, slots - 1].set(groups * boxes - 1).astype(jnp.int32)


def ragged_flags(key, groups, boxes, slots):
    first, second = jax.random.split(key)
    counts = jax.random.randint(first, (groups, boxes, 1), max(slots // 4, 1), slots + 1)
    scores = jax.random.randint(second, (groups, boxes, slots), 0, 1024) * slots + jnp.arange(slots, dtype=jnp.int32)
    ranks = jnp.argsort(jnp.argsort(scores, axis=-1, stable=True), axis=-1, stable=True)
    return (ranks < counts).astype(jnp.int32)


def draw_lists_a(key, part):
    key = jax.random.fold_in(key, 11)
    return near_ids(key, GROUPS, GLEAVES, P_A)


def draw_mask_a(key, part):
    key = jax.random.fold_in(key, 12)
    return ragged_flags(key, GROUPS, GLEAVES, P_A)


def draw_lists_b(key, part):
    key = jax.random.fold_in(key, 13)
    return near_ids(key, GROUPS, GB, P_B)


def draw_mask_b(key, part):
    key = jax.random.fold_in(key, 14)
    return ragged_flags(key, GROUPS, GB, P_B)


def draw_lists_c(key, part):
    key = jax.random.fold_in(key, 15)
    return any_ids(key, GROUPS, CPG, P_C)


def draw_mask_c(key, part):
    key = jax.random.fold_in(key, 16)
    return ragged_flags(key, GROUPS, CPG, P_C)


def level_of(rng, shape, shards, smallest, largest):
    gain, own = 1.0, jax.random.fold_in(rng, 6)
    for position, parts in shards:
        steps = jnp.exp(jax.random.uniform(jax.random.fold_in(own, position), (parts,), jnp.float32, smallest / len(shards), largest / len(shards)))
        gain = gain * jnp.repeat(steps, shape[position] // parts).reshape([-1 if axis == position else 1 for axis in range(len(shape))])
    return gain


def bell_draw(rng, extent, spread, limit, pieces=(), kind=jnp.bfloat16):
    array = jax.random.normal(rng, extent, jnp.float32) * spread
    if len(pieces) > 0:
        array = level_of(rng, extent, pieces, -0.22, 0.18) * array
    return jnp.clip(array, min=-limit, max=limit).astype(kind)


def setup_inputs(seed: int = 0) -> dict:
    key_list = jax.random.split(jax.random.key(seed), 14)
    values = bell_draw(key_list[0], (GROUPS, GLEAVES, RHS, PTS), 1.0, 6.0, ((0, 32), (1, 8)))
    basis = bell_draw(key_list[1], (GROUPS, GLEAVES, RANK, PTS), PTS ** -0.5, 0.375, ((0, 32), (1, 8)))
    transfer_b = bell_draw(key_list[2], (GROUPS, GB, RANK, 8 * RANK), (2 * RANK) ** -0.5, 0.5, ((0, 32), (1, 8)))
    transfer_c = bell_draw(key_list[3], (GROUPS, CPG, RANK, 8 * RANK), (2 * RANK) ** -0.5, 0.5, ((0, 32),))
    coupling_a = bell_draw(key_list[4], (GROUPS, GLEAVES, P_A, RANK * RANK), (RANK * P_A // 2) ** -0.5, 0.21875, ((0, 32), (1, 8)))
    lists_a = draw_lists_a(jax.random.fold_in(key_list[13], 71), 0)
    mask_a = draw_mask_a(jax.random.fold_in(key_list[13], 71), 0)
    coupling_b = bell_draw(key_list[7], (GROUPS, GB, P_B, RANK * RANK), (RANK * P_B // 2) ** -0.5, 0.21875, ((0, 32), (1, 8)))
    lists_b = draw_lists_b(jax.random.fold_in(key_list[13], 71), 0)
    mask_b = draw_mask_b(jax.random.fold_in(key_list[13], 71), 0)
    coupling_c = bell_draw(key_list[10], (GROUPS, CPG, P_C, RANK * RANK), (RANK * P_C // 2) ** -0.5, 0.21875, ((0, 32), (2, 8)))
    lists_c = draw_lists_c(jax.random.fold_in(key_list[13], 71), 0)
    mask_c = draw_mask_c(jax.random.fold_in(key_list[13], 71), 0)
    return {"values": values, "basis": basis, "transfer_b": transfer_b, "transfer_c": transfer_c, "coupling_a": coupling_a, "lists_a": lists_a, "mask_a": mask_a, "coupling_b": coupling_b, "lists_b": lists_b, "mask_b": mask_b, "coupling_c": coupling_c, "lists_c": lists_c, "mask_c": mask_c}


def couple(coupling, lists, mask, source):
    count, slots = lists.shape
    picked = jnp.take(source, lists, axis=0).astype(jnp.float32)
    picked = picked * mask.astype(jnp.float32)[:, :, None, None]
    blocks = coupling.reshape(count, slots, RANK, RANK).astype(jnp.float32)
    return jnp.einsum('npkm,npmr->nkr', blocks, picked)


def lift_leaves(pair):
    return jnp.einsum('nkp,nrp->nkr', pair[0].astype(jnp.float32), pair[1].astype(jnp.float32)).astype(jnp.bfloat16)


def spread_leaves(pair):
    return jnp.einsum('nkp,nkr->nrp', pair[0].astype(jnp.float32), pair[1].astype(jnp.float32)).astype(jnp.bfloat16)


def reference(values, basis, transfer_b, transfer_c, coupling_a, lists_a, mask_a, coupling_b, lists_b, mask_b, coupling_c, lists_c, mask_c):
    q_leaf = lax.map(lift_leaves, (basis, values))
    q_parent = jnp.einsum('gbkm,gbmr->gbkr', transfer_b.astype(jnp.float32), q_leaf.reshape(GROUPS, GB, 8 * RANK, RHS).astype(jnp.float32)).astype(jnp.bfloat16)
    q_grand = jnp.einsum('gckm,gcmr->gckr', transfer_c.astype(jnp.float32), q_parent.reshape(GROUPS, CPG, 8 * RANK, RHS).astype(jnp.float32)).astype(jnp.bfloat16)
    flat_leaf = q_leaf.reshape(GROUPS * GLEAVES, RANK, RHS)
    flat_parent = q_parent.reshape(GROUPS * GB, RANK, RHS)
    flat_grand = q_grand.reshape(GROUPS * CPG, RANK, RHS)
    y_grand = couple(coupling_c.reshape(GROUPS * CPG, P_C, RANK * RANK), lists_c.reshape(GROUPS * CPG, P_C), mask_c.reshape(GROUPS * CPG, P_C), flat_grand).astype(jnp.bfloat16)
    down_grand = jnp.einsum('gckm,gckr->gcmr', transfer_c.astype(jnp.float32), y_grand.reshape(GROUPS, CPG, RANK, RHS).astype(jnp.float32)).reshape(GROUPS, GB, RANK, RHS)
    near_parent = couple(coupling_b.reshape(GROUPS * GB, P_B, RANK * RANK), lists_b.reshape(GROUPS * GB, P_B), mask_b.reshape(GROUPS * GB, P_B), flat_parent).reshape(GROUPS, GB, RANK, RHS)
    y_parent = (near_parent + down_grand).astype(jnp.bfloat16)
    down_parent = jnp.einsum('gbkm,gbkr->gbmr', transfer_b.astype(jnp.float32), y_parent.astype(jnp.float32)).reshape(GROUPS, GLEAVES, RANK, RHS)

    def leaf_group(triple):
        return couple(triple[0], triple[1], triple[2], flat_leaf)

    near_leaf = lax.map(leaf_group, (coupling_a, lists_a, mask_a))
    y_leaf = (near_leaf + down_parent).astype(jnp.bfloat16)
    return lax.map(spread_leaves, (basis, y_leaf))
```

```python
import functools

import jax
import jax.numpy as jnp
from jax import lax
from jax.experimental import pallas as pl
from jax.experimental.pallas import tpu as pltpu
from jax.sharding import PartitionSpec as P

BF = jnp.bfloat16
F32 = jnp.float32
MESH = pl.DeviceIdType.MESH


def nt(a, b):
    return lax.dot_general(a, b, (((1,), (1,)), ((), ())), preferred_element_type=F32)


def nn(a, b):
    return jnp.dot(a, b, preferred_element_type=F32)


def grid_index(shape, dim):
    return lax.broadcasted_iota(jnp.int32, shape, dim)


def flag(condition):
    return jnp.where(condition, 1.0, 0.0)


def column(rows, height, stride):
    sub, lane = grid_index((height, 128), 0), grid_index((height, 128), 1)
    total = jnp.zeros((height, 128), F32)
    for place, row in enumerate(rows):
        width = row.shape[1]
        wide = jnp.concatenate([row.astype(F32), jnp.zeros((1, 128 - width), F32)], axis=1)
        hit = (lane == sub - place * stride) & (lane < width)
        total = total + jnp.where(hit, jnp.broadcast_to(wide, (height, 128)), 0.0)
    return jnp.sum(total, axis=1, keepdims=True).astype(jnp.int32)


def kernel(
    groups,
    values,
    basis,
    transfer_b,
    transfer_c,
    coupling_a,
    coupling_b,
    coupling_c,
    lists_a,
    mask_a,
    lists_b,
    mask_b,
    lists_c,
    mask_c,
    field,
    v_values,
    v_basis,
    v_tb,
    v_tc,
    v_ca,
    v_cb,
    v_cc,
    leaf_window,
    parent_window,
    grand_window,
    share_out,
    share_in,
    pick_a,
    picked,
    near,
    load_sem,
    y_send,
    y_recv,
    x_send,
    x_recv,
    mate_send,
    mate_recv,
    b_send,
    b_recv,
    bx_send,
    bx_recv,
    c_send,
    c_recv,
    s_send,
    s_recv,
):
    g = lax.axis_index("leaf")
    t = lax.axis_index("tel")
    y, core = t // 2, t % 2
    up, down = lax.rem(g + 1, groups), lax.rem(g + groups - 1, groups)

    loads = [
        pltpu.make_async_copy(source, target, load_sem.at[place])
        for place, (source, target) in enumerate(
            (
                (values, v_values),
                (basis, v_basis),
                (transfer_b, v_tb),
                (transfer_c, v_tc),
                (coupling_c, v_cc),
                (coupling_b, v_cb),
                (coupling_a, v_ca),
            )
        )
    ]
    for load in loads:
        load.start()

    barrier = pltpu.get_barrier_semaphore()

    def greet_group(d, carry):
        pl.semaphore_signal(
            barrier, inc=1, device_id={"tel": lax.rem(t + d, 8), "leaf": g}, device_id_type=MESH
        )
        return carry

    def greet_plane(d, carry):
        pl.semaphore_signal(
            barrier, inc=1, device_id={"tel": t, "leaf": lax.rem(g + d, groups)}, device_id_type=MESH
        )
        return carry

    lax.fori_loop(1, 8, greet_group, 0)
    lax.fori_loop(1, groups, greet_plane, 0)

    sub, lane = grid_index((8, 128), 0), grid_index((8, 128), 1)
    left = lane < 64
    even_left = (sub % 2 == 0) & left
    odd_right = (sub % 2 == 1) & (lane >= 64)

    loads[0].wait()
    loads[1].wait()
    placed, stacked = [], []
    for s in range(8):
        product = nt(v_values[32 * s : 32 * s + 32, :], v_basis[256 * s : 256 * s + 256, :])
        for h in range(2):
            first = product[16 * h : 16 * h + 8, 128 * h : 128 * h + 128]
            second = product[16 * h + 8 : 16 * h + 16, 128 * h : 128 * h + 128]
            placed.append(
                jnp.where(even_left, first, jnp.where(odd_right, pltpu.roll(first, 64, 1), 0.0))
            )
            placed.append(
                jnp.where(even_left, pltpu.roll(second, 64, 1), jnp.where(odd_right, second, 0.0))
            )
            stacked.append(jnp.where(left, first, second))
    placed = jnp.concatenate(placed, axis=0).astype(BF)
    row, col = grid_index((128, 256), 0), grid_index((128, 256), 1)
    order = flag((row % 32 == col // 8) & (row // 32 == (col % 8) // 2)).astype(BF)
    own_slot = 8 + core * 4 + y
    leaf_window[own_slot] = nn(order, placed).astype(BF)

    loads[2].wait()
    lifted = []
    for b in range(4):
        children = jnp.concatenate(stacked[4 * b : 4 * b + 4], axis=1).astype(BF)
        lifted.append(nt(children, v_tb[64 * b : 64 * b + 64, :]))
    parent_window[8 + t] = jnp.concatenate(
        [jnp.concatenate(lifted[0:2], axis=1), jnp.concatenate(lifted[2:4], axis=1)], axis=0
    ).astype(BF)

    pl.semaphore_wait(barrier, 7 + groups - 1)

    def send(source, target, send_sem, recv_sem, tel, leaf):
        copy = pltpu.make_async_remote_copy(
            src_ref=source,
            dst_ref=target,
            send_sem=send_sem,
            recv_sem=recv_sem,
            device_id={"tel": tel, "leaf": leaf},
            device_id_type=MESH,
        )
        copy.start()
        return copy

    sent = []
    for d in range(1, 8):
        block = parent_window.at[8 + t]
        sent.append(send(block, block, b_send.at[d - 1], b_recv.at[0], lax.rem(t + d, 8), g))

    mate = t + 1 - 2 * core

    def spread(slot, place):
        block = leaf_window.at[slot]
        sent.append(
            send(block, leaf_window.at[slot - 8], x_send.at[place], x_recv.at[place], t, up)
        )
        sent.append(
            send(block, leaf_window.at[slot + 8], x_send.at[4 + place], x_recv.at[4 + place], t, down)
        )
        sent.append(send(block, block, mate_send.at[place], mate_recv.at[place], mate, g))

    own = leaf_window.at[own_slot]
    for d in range(1, 4):
        sent.append(
            send(own, own, y_send.at[d - 1], y_recv.at[d - 1], lax.rem(y + d, 4) * 2 + core, g)
        )
    spread(own_slot, 0)

    local = lists_a[...] - (g - 1) * 256
    inner = local % 256
    slot = (local // 256) * 8 + ((inner // 32) % 2) * 4 + inner // 64
    place = jnp.where(mask_a[...] == 1, slot * 32 + inner % 32, -1)
    lane24 = grid_index((24, 128), 1)
    for pair in range(16):
        rows = []
        for n in (2 * pair, 2 * pair + 1):
            wide = jnp.broadcast_to(place[:, n : n + 1], (24, 128)) - lane24
            rows.append(jnp.concatenate([flag(wide == 128 * k) for k in range(6)], axis=1))
        pick_a[48 * pair : 48 * pair + 48, :] = jnp.concatenate(rows, axis=0).astype(BF)

    def received(ref, sem):
        pltpu.make_async_copy(ref, ref, sem).wait()

    received(parent_window.at[pl.ds(0, 7)], b_recv.at[0])
    loads[3].wait()
    lifted = []
    for c in range(4):
        one = parent_window[8 + 2 * c].astype(F32)
        two = parent_window[9 + 2 * c].astype(F32)
        children = jnp.concatenate([one[0:8], one[8:16], two[0:8], two[8:16]], axis=1).astype(BF)
        lifted.append(nt(children, v_tc[64 * c : 64 * c + 64, :]))
    grand_window[g] = jnp.concatenate(
        [jnp.concatenate(lifted[0:2], axis=1), jnp.concatenate(lifted[2:4], axis=1)], axis=0
    ).astype(BF)

    def grand_copy(d):
        block = grand_window.at[g]
        return pltpu.make_async_remote_copy(
            src_ref=block,
            dst_ref=block,
            send_sem=c_send.at[0],
            recv_sem=c_recv.at[0],
            device_id={"tel": t, "leaf": lax.rem(g + d, groups)},
            device_id_type=MESH,
        )

    def start_grand(d, carry):
        grand_copy(d).start()
        return carry

    lax.fori_loop(1, groups, start_grand, 0)
    group_parents = parent_window.at[pl.ds(8, 8)]
    sent.append(send(group_parents, parent_window.at[pl.ds(0, 8)], bx_send.at[0], bx_recv.at[0], t, up))
    sent.append(
        send(group_parents, parent_window.at[pl.ds(16, 8)], bx_send.at[1], bx_recv.at[1], t, down)
    )

    for d in range(1, 4):
        source = 8 + core * 4 + lax.rem(y + 4 - d, 4)
        received(leaf_window.at[source], y_recv.at[d - 1])
        spread(source, d)

    choose_b, half_b = [], []
    lane384 = grid_index((8, 384), 1)
    for n in range(4):
        entry = column([lists_b[n : n + 1, :]], 24, 0) - (g - 1) * 32
        valid = column([mask_b[n : n + 1, :]], 24, 0)
        base = jnp.where(valid == 1, (entry // 2) * 8, -1000)
        for i in range(3):
            wide = jnp.broadcast_to(base[8 * i : 8 * i + 8], (8, 384)) - lane384
            choose_b.extend(flag(wide == -r) for r in range(8))
            half_b.append(jnp.broadcast_to(entry[8 * i : 8 * i + 8] % 2, (8, 128)) == lane // 64)
    choose_b = jnp.concatenate(choose_b, axis=0).astype(BF)
    grand_rows = 16 * groups
    entry = column([lists_c[p] for p in range(3)], 16, 4)
    valid = column([mask_c[p] for p in range(3)], 16, 4)
    base = jnp.where(valid == 1, (entry // 2) * 8, -1000)
    wide = jnp.broadcast_to(base, (16, grand_rows)) - grid_index((16, grand_rows), 1)
    choose_c = jnp.concatenate([flag(wide == -r) for r in range(8)], axis=0).astype(BF)
    half_c = jnp.broadcast_to(entry % 2, (16, 128)) == grid_index((16, 128), 1) // 64

    row, col = grid_index((128, 256), 0), grid_index((128, 256), 1)
    same_p = row % 8 == col % 8
    row, col = grid_index((32, 256), 0), grid_index((32, 256), 1)
    fold = flag(
        (row // 16 == col // 128) & (row % 8 == (col // 16) % 8) & ((row // 8) % 2 == (col // 8) % 2)
    ).astype(BF)
    diagonal4 = row // 8 == col // 64
    row, col = grid_index((512, 256), 0), grid_index((512, 256), 1)
    expand = flag(col % 64 == 2 * ((row % 256) // 8) + row // 256).astype(BF)
    row, col = grid_index((32, 128), 0), grid_index((32, 128), 1)
    diagonal2 = (row // 8) % 2 == col // 64
    row, col = grid_index((16, 128), 0), grid_index((16, 128), 1)
    halves = flag(row // 8 == col // 64).astype(BF)

    for d in range(4):
        source = core * 4 + lax.rem(y + 4 - d, 4)
        for side in range(2):
            block = leaf_window.at[source + 16 * side]
            received(block, x_recv.at[4 * side + d])
            k = 4 + 2 * d + side
            sent.append(send(block, block, mate_send.at[k], mate_recv.at[k], mate, g))

    received(grand_window.at[pl.ds(0, groups - 1)], c_recv.at[0])
    loads[4].wait()
    found = nn(choose_c, grand_window[...].reshape(grand_rows, 128))
    lane16 = grid_index((16, 128), 1)
    rows = []
    for r in range(8):
        one = found[16 * r : 16 * r + 16]
        both = jnp.where(half_c, one, pltpu.roll(one, 64, 1))
        rows.append(jnp.where(lane16 < 64, both, 0.0))
        rows.append(jnp.where(lane16 < 64, 0.0, both))
    full = nt(jnp.concatenate(rows, axis=0).astype(BF), v_cc[...])
    row, col = grid_index((256, 512), 0), grid_index((256, 512), 1)
    full = jnp.where(row % 16 == col % 16, full, 0.0).astype(BF)
    row, col = grid_index((64, 256), 0), grid_index((64, 256), 1)
    fold_c = flag(
        (row // 32 == (col // 16) % 2) & ((row // 8) % 4 == col % 4) & (row % 8 == col // 32)
    ).astype(BF)
    folded = nn(fold_c, full).astype(BF)
    row, col = grid_index((512, 128), 0), grid_index((512, 128), 1)
    share = nn(folded[0:32], flag(col % 64 == 2 * (row // 16)).astype(BF)) + nn(
        folded[32:64], flag(col % 64 == 2 * (row // 16) + 1).astype(BF)
    )
    for c in range(4):
        share_out[c] = share[8 * c : 8 * c + 8]
    for d in range(1, 8):
        target = lax.rem(t + d, 8)
        sent.append(
            send(share_out.at[target // 2], share_in.at[d - 1], s_send.at[d - 1], s_recv.at[0], target, g)
        )

    def couple(lhs, coupling):
        wide = jnp.concatenate([coupling[256 * i : 256 * i + 256] for i in range(3)], axis=1)
        return jnp.where(same_p, nt(lhs, wide), 0.0).astype(BF)

    def folded_rows(pair):
        z = nn(fold, jnp.concatenate(pair, axis=0)).astype(F32)
        return [jnp.concatenate([z[16 * j : 16 * j + 8], z[16 * j + 8 : 16 * j + 16]], axis=1) for j in (0, 1)]

    received(parent_window.at[pl.ds(0, 8)], bx_recv.at[0])
    received(parent_window.at[pl.ds(16, 8)], bx_recv.at[1])
    loads[5].wait()
    found = nn(choose_b, parent_window[...].reshape(384, 128))
    rows, pair = [], []
    for n in range(4):
        lanes = []
        for i in range(3):
            pieces = []
            for r in range(8):
                at = 8 * ((n * 3 + i) * 8 + r)
                one = found[at : at + 8]
                both = jnp.where(half_b[n * 3 + i], one, pltpu.roll(one, 64, 1))
                pieces.append(jnp.concatenate([both, both], axis=0).astype(BF) * halves)
            lanes.append(jnp.concatenate(pieces, axis=0))
        pair.append(couple(jnp.concatenate(lanes, axis=1), v_cb[n]))
        if n % 2:
            rows.extend(folded_rows(pair))
            pair = []
    near_b = nn(jnp.concatenate(rows, axis=0).astype(BF), expand[:, 0:128])

    for k in range(4):
        if k == 0:
            block = leaf_window.at[8 + (1 - core) * 4 + y]
        else:
            block = leaf_window.at[8 + (1 - core) * 4 + lax.rem(y + 4 - k, 4)]
        received(block, mate_recv.at[k])
    for d in range(4):
        source = (1 - core) * 4 + lax.rem(y + 4 - d, 4)
        for side in range(2):
            received(leaf_window.at[source + 16 * side], mate_recv.at[4 + 2 * d + side])
    loads[6].wait()
    for half in range(2):
        window = jnp.concatenate(
            [
                leaf_window[:, 32 * k : 32 * k + 32, :].reshape(768, 128)
                for k in (2 * half, 2 * half + 1)
            ],
            axis=1,
        )
        picked[:, 256 * half : 256 * half + 256] = nn(pick_a[...], window)

    def leaf_stack(s, carry):
        rows, pair = [], []
        for j in range(4):
            n = 4 * s + j
            lanes = []
            for i in range(3):
                eight = picked[pl.ds(pl.multiple_of(24 * n + 8 * i, 8), 8), :]
                pieces = []
                for k in range(4):
                    one = eight[:, 128 * k : 128 * k + 128]
                    turned = pltpu.roll(one, 64, 1)
                    pieces.append(jnp.concatenate([one, turned], axis=0).astype(BF) * halves)
                    pieces.append(jnp.concatenate([turned, one], axis=0).astype(BF) * halves)
                lanes.append(jnp.concatenate(pieces, axis=0))
            pair.append(couple(jnp.concatenate(lanes, axis=1), v_ca.at[n]))
            if j % 2:
                rows.extend(folded_rows(pair))
                pair = []
        near[s] = nn(jnp.concatenate(rows, axis=0).astype(BF), expand)
        return carry

    lax.fori_loop(0, 8, leaf_stack, 0)

    received(share_in, s_recv.at[0])
    total = share_out[y]
    for d in range(7):
        total = total + share_in[d]
    y_c = total[:, 0:64].astype(BF)
    spread_c = nn(y_c, v_tc[pl.ds(pl.multiple_of(64 * y, 64), 64), :])
    own_down = jnp.where(core == 0, spread_c[:, 0:256], spread_c[:, 256:512])
    for h in range(2):
        part = own_down[:, 128 * h : 128 * h + 128]
        part = near_b[16 * h : 16 * h + 16] + jnp.concatenate([part, part], axis=0)
        y_b = jnp.where(diagonal2[0:16], part, 0.0).astype(BF)
        spread_b = nn(y_b, v_tb[128 * h : 128 * h + 128, :])
        for j in range(2):
            for k in range(2):
                s = 4 * h + 2 * j + k
                part = spread_b[8 * j : 8 * j + 8, 256 * k : 256 * k + 256]
                part = near[s] + jnp.concatenate([part] * 4, axis=0)
                y_a = jnp.where(diagonal4, part, 0.0).astype(BF)
                field[32 * s : 32 * s + 32, :] = nn(y_a, v_basis[256 * s : 256 * s + 256, :]).astype(BF)

    for copy in sent:
        copy.wait_send()
    pltpu.make_async_copy(
        grand_window.at[pl.ds(0, groups - 1)], grand_window.at[pl.ds(0, groups - 1)], c_send.at[0]
    ).wait()


def tiles(coupling):
    boxes = coupling.shape[0]
    split = coupling.reshape(boxes, 3, 8, 32, 128)
    return split.transpose(0, 1, 3, 2, 4).reshape(boxes, 768, 128)


def on_device(
    values,
    basis,
    transfer_b,
    transfer_c,
    coupling_a,
    lists_a,
    mask_a,
    coupling_b,
    lists_b,
    mask_b,
    coupling_c,
    lists_c,
    mask_c,
):
    groups = lax.axis_size("leaf")
    grand = coupling_c[0].transpose(1, 0, 2).reshape(12, 32, 128)
    grand = jnp.pad(grand, ((0, 4), (0, 0), (0, 0))).transpose(1, 0, 2).reshape(512, 128)
    operands = (
        values.reshape(256, 256),
        basis.reshape(2048, 256),
        transfer_b.reshape(256, 512),
        transfer_c.reshape(256, 512),
        tiles(coupling_a[0]),
        tiles(coupling_b[0]),
        grand,
        lists_a[0].T,
        mask_a[0].T,
        lists_b[0],
        mask_b[0],
        lists_c.transpose(2, 0, 1),
        mask_c.transpose(2, 0, 1),
    )
    anywhere = pl.BlockSpec(memory_space=pl.ANY)
    local = pl.BlockSpec(memory_space=pltpu.VMEM)
    dma = pltpu.SemaphoreType.DMA
    field = pl.pallas_call(
        functools.partial(kernel, groups),
        out_shape=jax.ShapeDtypeStruct((256, 256), BF),
        in_specs=[anywhere] * 7 + [local] * 6,
        out_specs=local,
        scratch_shapes=[pltpu.VMEM(x.shape, x.dtype) for x in operands[:7]]
        + [
            pltpu.VMEM((24, 128, 128), BF),
            pltpu.VMEM((24, 16, 128), BF),
            pltpu.VMEM((groups, 16, 128), BF),
            pltpu.VMEM((4, 8, 128), F32),
            pltpu.VMEM((7, 8, 128), F32),
            pltpu.VMEM((768, 768), BF),
            pltpu.VMEM((768, 512), F32),
            pltpu.VMEM((8, 32, 256), F32),
        ]
        + [dma((k,)) for k in (7, 3, 3, 8, 8, 12, 12, 7, 1, 2, 2, 1, 1, 7, 1)],
        compiler_params=pltpu.CompilerParams(
            collective_id=0, has_side_effects=True, vmem_limit_bytes=40 * 1024 * 1024
        ),
        cost_estimate=pl.CostEstimate(flops=5_000_000_000, bytes_accessed=10_000_000, transcendentals=0),
        name="far_field",
    )(*operands)
    return field.reshape(1, 32, 8, 256)


def solution(mesh):
    in_specs = (
        P("leaf", "tel", None, None),
        P("leaf", "tel", None, None),
        P("leaf", "tel", None, None),
        P("leaf", None, None, None),
        P("leaf", "tel", None, None),
        P("leaf", "tel", None),
        P("leaf", "tel", None),
        P("leaf", "tel", None, None),
        P("leaf", "tel", None),
        P("leaf", "tel", None),
        P("leaf", None, "tel", None),
        P("leaf", None, "tel"),
        P("leaf", None, "tel"),
    )
    out_specs = P("leaf", "tel", None, None)
    return jax.shard_map(
        on_device, mesh=mesh, in_specs=in_specs, out_specs=out_specs, check_vma=False
    )
```

```python
import functools

import jax
import jax.numpy as jnp
from jax import lax
from jax.experimental import pallas as pl
from jax.experimental.pallas import tpu as pltpu
from jax.sharding import PartitionSpec as P

BF = jnp.bfloat16
F32 = jnp.float32
MESH = pl.DeviceIdType.MESH


def nt(a, b):
    return lax.dot_general(a, b, (((1,), (1,)), ((), ())), preferred_element_type=F32)


def nn(a, b):
    return jnp.dot(a, b, preferred_element_type=F32)


def grid_index(shape, dim):
    return lax.broadcasted_iota(jnp.int32, shape, dim)


def flag(condition):
    return jnp.where(condition, 1.0, 0.0)


def far_first(depth):
    offsets = [(dz, dx) for dz in range(depth) for dx in range(4) if dz or dx]
    return sorted(offsets, key=lambda o: -(min(o[0], depth - o[0]) + min(o[1], 4 - o[1])))


def column(rows, height, stride):
    sub, lane = grid_index((height, 128), 0), grid_index((height, 128), 1)
    total = jnp.zeros((height, 128), F32)
    for place, row in enumerate(rows):
        width = row.shape[1]
        wide = jnp.concatenate([row.astype(F32), jnp.zeros((1, 128 - width), F32)], axis=1)
        hit = (lane == sub - place * stride) & (lane < width)
        total = total + jnp.where(hit, jnp.broadcast_to(wide, (height, 128)), 0.0)
    return jnp.sum(total, axis=1, keepdims=True).astype(jnp.int32)


def kernel(
    groups,
    values,
    basis,
    transfer_b,
    transfer_c,
    coupling_a,
    coupling_b,
    coupling_c,
    lists_a,
    mask_a,
    lists_b,
    mask_b,
    lists_c,
    mask_c,
    field,
    v_values,
    v_basis,
    v_tb,
    v_tc,
    v_ca,
    v_cb,
    v_cc,
    v_lists_a,
    v_mask_a,
    v_lists_b,
    v_mask_b,
    v_lists_c,
    v_mask_c,
    leaf_window,
    parent_window,
    grand_window,
    share_out,
    share_in,
    pick_a,
    picked,
    left_side,
    products,
    folded,
    near,
    load_sem,
    y_send,
    y_recv,
    x_send,
    x_recv,
    mate_send,
    mate_recv,
    b_send,
    b_recv,
    bx_send,
    bx_recv,
    c_send,
    c_recv,
    here,
    s_send,
    s_recv,
):
    g = lax.axis_index("leaf")
    t = lax.axis_index("tel")
    y, core = t // 2, t % 2
    depth = groups // 4

    def group_at(dz, dx):
        return lax.rem(g // 4 + dz, depth) * 4 + lax.rem(g + dx, 4)

    up, down = lax.rem(g + 1, groups), lax.rem(g + groups - 1, groups)

    loads = [
        pltpu.make_async_copy(source, target, load_sem.at[place])
        for place, (source, target) in enumerate(
            (
                (values, v_values),
                (basis, v_basis),
                (transfer_b, v_tb),
                (transfer_c, v_tc),
                (coupling_c, v_cc),
                (coupling_b, v_cb),
                (coupling_a, v_ca),
                (lists_a, v_lists_a),
                (mask_a, v_mask_a),
                (lists_b, v_lists_b),
                (mask_b, v_mask_b),
                (lists_c, v_lists_c),
                (mask_c, v_mask_c),
            )
        )
    ]
    for load in loads[0:3]:
        load.start()

    barrier = pltpu.get_barrier_semaphore()

    def greet_group(d, carry):
        pl.semaphore_signal(
            barrier, inc=1, device_id={"tel": lax.rem(t + d, 8), "leaf": g}, device_id_type=MESH
        )
        return carry

    lax.fori_loop(1, 8, greet_group, 0)
    z = g // 4

    def signal_plane(semaphore, offset, along_x):
        @pl.when((z + offset >= 0) & (z + offset < depth))
        def _():
            for dx in along_x:
                target = (z + offset) * 4 + lax.rem(g + dx, 4)
                pl.semaphore_signal(
                    semaphore, inc=1, device_id={"tel": t, "leaf": target}, device_id_type=MESH
                )

    def planes(*offsets):
        return sum(((z + o >= 0) & (z + o < depth)).astype(jnp.int32) for o in offsets)

    signal_plane(barrier, 0, (1, 2, 3))
    signal_plane(barrier, 1, range(4))
    signal_plane(barrier, -1, range(4))

    sub, lane = grid_index((8, 128), 0), grid_index((8, 128), 1)
    left = lane < 64
    even_left = (sub % 2 == 0) & left
    odd_right = (sub % 2 == 1) & (lane >= 64)

    for end, first in ((0, 0), (groups - 1, 16)):

        @pl.when(g == end)
        def _():
            leaf_window[first : first + 8] = jnp.zeros((8, 128, 128), BF)
            parent_window[first : first + 8] = jnp.zeros((8, 16, 128), BF)

    loads[0].wait()
    loads[1].wait()
    for load in loads[7:13] + loads[3:7]:
        load.start()
    pl.semaphore_wait(barrier, 10 + 4 * planes(-1, 1))
    for offset in (-1, 1):
        signal_plane(here.at[0], offset, (0,))

    placed, stacked = [], []
    for s in range(8):
        product = nt(v_values[32 * s : 32 * s + 32, :], v_basis[256 * s : 256 * s + 256, :])
        for h in range(2):
            first = product[16 * h : 16 * h + 8, 128 * h : 128 * h + 128]
            second = product[16 * h + 8 : 16 * h + 16, 128 * h : 128 * h + 128]
            placed.append(
                jnp.where(even_left, first, jnp.where(odd_right, pltpu.roll(first, 64, 1), 0.0))
            )
            placed.append(
                jnp.where(even_left, pltpu.roll(second, 64, 1), jnp.where(odd_right, second, 0.0))
            )
            stacked.append(jnp.where(left, first, second))
    placed = jnp.concatenate(placed, axis=0).astype(BF)
    row, col = grid_index((128, 256), 0), grid_index((128, 256), 1)
    order = flag((row % 32 == col // 8) & (row // 32 == (col % 8) // 2)).astype(BF)
    own_slot = 8 + core * 4 + y
    leaf_window[own_slot] = nn(order, placed).astype(BF)

    loads[2].wait()
    lifted = []
    for b in range(4):
        children = jnp.concatenate(stacked[4 * b : 4 * b + 4], axis=1).astype(BF)
        lifted.append(nt(children, v_tb[64 * b : 64 * b + 64, :]))
    parent_window[8 + t] = jnp.concatenate(
        [jnp.concatenate(lifted[0:2], axis=1), jnp.concatenate(lifted[2:4], axis=1)], axis=0
    ).astype(BF)

    def send(source, target, send_sem, recv_sem, tel, leaf, when=True):
        copy = pltpu.make_async_remote_copy(
            src_ref=source,
            dst_ref=target,
            send_sem=send_sem,
            recv_sem=recv_sem,
            device_id={"tel": tel, "leaf": leaf},
            device_id_type=MESH,
        )
        pl.when(when)(copy.start)
        return copy, when

    sent = []
    for d in range(1, 8):
        block = parent_window.at[8 + t]
        sent.append(send(block, block, b_send.at[d - 1], b_recv.at[0], lax.rem(t + d, 8), g))

    mate = t + 1 - 2 * core

    has_up, has_down = g < groups - 1, g > 0

    def spread(slot, place):
        block = leaf_window.at[slot]
        sent.append(
            send(block, leaf_window.at[slot - 8], x_send.at[place], x_recv.at[place], t, up, has_up)
        )
        sent.append(
            send(
                block, leaf_window.at[slot + 8], x_send.at[4 + place], x_recv.at[4 + place], t, down, has_down
            )
        )
        sent.append(send(block, block, mate_send.at[place], mate_recv.at[place], mate, g))

    own = leaf_window.at[own_slot]
    for d in range(1, 4):
        sent.append(
            send(own, own, y_send.at[d - 1], y_recv.at[d - 1], lax.rem(y + d, 4) * 2 + core, g)
        )
    spread(own_slot, 0)

    pl.semaphore_wait(here.at[0], planes(-1, 1))
    for offset in (-2, 2):
        signal_plane(here.at[1], offset, (0,))

    loads[7].wait()
    loads[8].wait()
    local = v_lists_a[...] - (g - 1) * 256
    inner = local % 256
    slot = (local // 256) * 8 + ((inner // 32) % 2) * 4 + inner // 64
    place = jnp.where(v_mask_a[...] == 1, slot * 32 + inner % 32, -1)
    lane24 = grid_index((24, 128), 1)
    for pair in range(16):
        rows = []
        for n in (2 * pair, 2 * pair + 1):
            wide = jnp.broadcast_to(place[:, n : n + 1], (24, 128)) - lane24
            rows.append(jnp.concatenate([flag(wide == 128 * k) for k in range(6)], axis=1))
        pick_a[48 * pair : 48 * pair + 48, :] = jnp.concatenate(rows, axis=0).astype(BF)

    def received(ref, sem, when=True):
        pl.when(when)(pltpu.make_async_copy(ref, ref, sem).wait)

    received(parent_window.at[pl.ds(0, 7)], b_recv.at[0])
    loads[3].wait()
    lifted = []
    for c in range(4):
        one = parent_window[8 + 2 * c].astype(F32)
        two = parent_window[9 + 2 * c].astype(F32)
        children = jnp.concatenate([one[0:8], one[8:16], two[0:8], two[8:16]], axis=1).astype(BF)
        lifted.append(nt(children, v_tc[64 * c : 64 * c + 64, :]))
    grand_window[g] = jnp.concatenate(
        [jnp.concatenate(lifted[0:2], axis=1), jnp.concatenate(lifted[2:4], axis=1)], axis=0
    ).astype(BF)

    block = grand_window.at[g]
    grand_copies = [
        pltpu.make_async_remote_copy(
            src_ref=block,
            dst_ref=block,
            send_sem=c_send.at[k],
            recv_sem=c_recv.at[0],
            device_id={"tel": t, "leaf": group_at(dz, dx)},
            device_id_type=MESH,
        )
        for k, (dz, dx) in enumerate(far_first(depth))
    ]
    sent.extend((copy, True) for copy in grand_copies)

    def send_grand():
        pl.semaphore_wait(here.at[2], planes(-4, 4))
        for copy in grand_copies:
            copy.start()

    group_parents = parent_window.at[pl.ds(8, 8)]
    sent.append(
        send(group_parents, parent_window.at[pl.ds(0, 8)], bx_send.at[0], bx_recv.at[0], t, up, has_up)
    )
    sent.append(
        send(group_parents, parent_window.at[pl.ds(16, 8)], bx_send.at[1], bx_recv.at[1], t, down, has_down)
    )

    for d in range(1, 4):
        source = 8 + core * 4 + lax.rem(y + 4 - d, 4)
        received(leaf_window.at[source], y_recv.at[d - 1])
        spread(source, d)

    pl.semaphore_wait(here.at[1], planes(-2, 2))
    for offset in (-4, 4):
        signal_plane(here.at[2], offset, (0,))
    pl.when(z >= depth // 2)(send_grand)

    for load in loads[9:13]:
        load.wait()
    choose_b, half_b = [], []
    lane384 = grid_index((8, 384), 1)
    for n in range(4):
        entry = column([v_lists_b[n : n + 1, :]], 24, 0) - (g - 1) * 32
        valid = column([v_mask_b[n : n + 1, :]], 24, 0)
        base = jnp.where(valid == 1, (entry // 2) * 8, -1000)
        for i in range(3):
            wide = jnp.broadcast_to(base[8 * i : 8 * i + 8], (8, 384)) - lane384
            choose_b.extend(flag(wide == -r) for r in range(8))
            half_b.append(jnp.broadcast_to(entry[8 * i : 8 * i + 8] % 2, (8, 128)) == lane // 64)
    choose_b = jnp.concatenate(choose_b, axis=0).astype(BF)

    for d in range(4):
        source = core * 4 + lax.rem(y + 4 - d, 4)
        for side in range(2):
            block = leaf_window.at[source + 16 * side]
            there = (has_down, has_up)[side]
            received(block, x_recv.at[4 * side + d], there)
            k = 4 + 2 * d + side
            sent.append(send(block, block, mate_send.at[k], mate_recv.at[k], mate, g, there))

    pl.when(z < depth // 2)(send_grand)

    loads[4].wait()
    codes = jnp.zeros((4, 128), F32)
    lane4 = grid_index((4, 128), 1)
    for p in range(3):
        entry = column([v_lists_c[p]], 4, 0)
        valid = column([v_mask_c[p]], 4, 0)
        code = jnp.where(valid == 1, entry, -1).astype(F32)
        codes = jnp.where(lane4 == p, jnp.broadcast_to(code, (4, 128)), codes)
    codes = jnp.concatenate([codes, jnp.zeros((4, 4096 - 128), F32)], axis=1)
    upper = jnp.concatenate([v_cc[0].astype(F32), v_cc[1].astype(F32)], axis=0)
    lower = jnp.concatenate([v_cc[2].astype(F32), codes], axis=0)
    blocks_c = []
    for k in range(32):
        blocks_c.append(upper[:, 128 * k : 128 * k + 128])
        blocks_c.append(lower[:, 128 * k : 128 * k + 128])
    blocks_c = jnp.concatenate(blocks_c, axis=0).astype(BF)
    row, col = grid_index((512, 512), 0), grid_index((512, 512), 1)
    regroup = flag((row // 128 == col % 4) & (row % 4 == (col % 16) // 4) & ((row % 128) // 4 == col // 16))
    blocks_c = nn(regroup.astype(BF), blocks_c).astype(BF)
    for c in range(4):
        share_out[c] = blocks_c[128 * c : 128 * c + 128]
    share_in[t] = share_out[y]
    for d in range(1, 8):
        target = lax.rem(t + d, 8)
        sent.append(
            send(share_out.at[target // 2], share_in.at[t], s_send.at[d - 1], s_recv.at[0], target, g)
        )

    row, col = grid_index((128, 256), 0), grid_index((128, 256), 1)
    same_p = row % 8 == col % 8
    row, col = grid_index((32, 256), 0), grid_index((32, 256), 1)
    fold = flag(
        ((row // 8) % 2 == col // 128) & (row % 8 == (col // 16) % 8) & (row // 16 == (col // 8) % 2)
    ).astype(BF)
    diagonal4 = row // 8 == col // 64
    row, col = grid_index((512, 256), 0), grid_index((512, 256), 1)
    expand = flag(col % 64 == 2 * ((row % 256) // 8) + row // 256).astype(BF)
    row, col = grid_index((32, 128), 0), grid_index((32, 128), 1)
    diagonal2 = (row // 8) % 2 == col // 64
    row, col = grid_index((16, 128), 0), grid_index((16, 128), 1)
    halves = flag(row // 8 == col // 64).astype(BF)

    def couple(lhs, coupling):
        wide = jnp.concatenate([coupling[256 * i : 256 * i + 256] for i in range(3)], axis=1)
        return jnp.where(same_p, nt(lhs, wide), 0.0).astype(BF)

    def fold_pair(pair):
        both = nn(fold, pair)
        return jnp.concatenate([both[0:16], both[16:32]], axis=1).astype(BF)

    received(parent_window.at[pl.ds(0, 8)], bx_recv.at[0], has_down)
    received(parent_window.at[pl.ds(16, 8)], bx_recv.at[1], has_up)
    loads[5].wait()
    found = nn(choose_b, parent_window[...].reshape(384, 128))
    rows, pair = [], []
    for n in range(4):
        lanes = []
        for i in range(3):
            pieces = []
            for r in range(8):
                at = 8 * ((n * 3 + i) * 8 + r)
                one = found[at : at + 8]
                both = jnp.where(half_b[n * 3 + i], one, pltpu.roll(one, 64, 1))
                pieces.append(jnp.concatenate([both, both], axis=0).astype(BF) * halves)
            lanes.append(jnp.concatenate(pieces, axis=0))
        pair.append(couple(jnp.concatenate(lanes, axis=1), v_cb[n]))
        if n % 2:
            rows.append(fold_pair(jnp.concatenate(pair, axis=0)))
            pair = []
    near_b = nn(jnp.concatenate(rows, axis=0), expand[:, 0:128])

    for k in range(4):
        if k == 0:
            block = leaf_window.at[8 + (1 - core) * 4 + y]
        else:
            block = leaf_window.at[8 + (1 - core) * 4 + lax.rem(y + 4 - k, 4)]
        received(block, mate_recv.at[k])
    for d in range(4):
        source = (1 - core) * 4 + lax.rem(y + 4 - d, 4)
        for side in range(2):
            received(
                leaf_window.at[source + 16 * side], mate_recv.at[4 + 2 * d + side], (has_down, has_up)[side]
            )
    loads[6].wait()
    for half in range(2):
        window = jnp.concatenate(
            [
                leaf_window[:, 32 * k : 32 * k + 32, :].reshape(768, 128)
                for k in (2 * half, 2 * half + 1)
            ],
            axis=1,
        )
        picked[:, 256 * half : 256 * half + 256] = nn(pick_a[...], window)

    def build(n, carry):
        lanes = []
        for i in range(3):
            eight = picked[pl.ds(pl.multiple_of(24 * n + 8 * i, 8), 8), :]
            pieces = []
            for k in range(4):
                one = eight[:, 128 * k : 128 * k + 128]
                turned = pltpu.roll(one, 64, 1)
                pieces.append(jnp.concatenate([one, turned], axis=0).astype(BF) * halves)
                pieces.append(jnp.concatenate([turned, one], axis=0).astype(BF) * halves)
            lanes.append(jnp.concatenate(pieces, axis=0))
        left_side[n] = jnp.concatenate(lanes, axis=1)
        return carry

    def multiply(n, carry):
        products[n] = couple(left_side[n], v_ca.at[n])
        return carry

    def fold_products(pair, carry):
        rows = products[pl.ds(2 * pair, 2)].reshape(256, 256)
        folded[pl.ds(pl.multiple_of(16 * pair, 16), 16), :] = fold_pair(rows)
        return carry

    lax.fori_loop(0, 32, build, 0, unroll=4)
    lax.fori_loop(0, 32, multiply, 0, unroll=4)
    lax.fori_loop(0, 16, fold_products, 0, unroll=4)
    near[...] = nn(folded[...], expand)

    received(share_in.at[pl.ds(0, 7)], s_recv.at[0])
    grand_rows = 16 * groups
    row, lane32 = grid_index((32, 128), 0), grid_index((32, 128), 1)
    choose_c, half_c = [], []
    for source in range(8):
        code = jnp.broadcast_to(share_in[source, 0:16, :].astype(F32)[3:4], (32, 128))
        code = jnp.sum(jnp.where(lane32 == row // 8, code, 0.0), axis=1, keepdims=True).astype(jnp.int32)
        row1 = grid_index((32, 1), 0)
        base = jnp.where((code >= 0) & (row1 < 24), (code // 2) * 8 + row1 % 8, -1000)
        hit = jnp.broadcast_to(base, (32, grand_rows)) == grid_index((32, grand_rows), 1)
        choose_c.append(flag(hit))
        half_c.append(jnp.broadcast_to(code % 2, (32, 128)) == lane32 // 64)
    choose_c = jnp.concatenate(choose_c, axis=0).astype(BF)
    half_c = jnp.concatenate(half_c, axis=0)
    blocks_c = jnp.concatenate([share_in[source] for source in range(8)], axis=1)
    row, col = grid_index((64, 128), 0), grid_index((64, 128), 1)
    same_c = row // 16 == col % 4
    row, col = grid_index((256, 64), 0), grid_index((256, 64), 1)
    expand_c = flag(col == 2 * ((row % 128) // 4) + row // 128).astype(BF)

    received(grand_window.at[pl.ds(0, groups - 1)], c_recv.at[0])
    found = nn(choose_c, grand_window[...].reshape(grand_rows, 128))
    found = jnp.where(half_c, found, pltpu.roll(found, 64, 1))
    lanes = []
    for source in range(8):
        pieces = []
        for e in range(4):
            one = found[32 * source + 8 * e : 32 * source + 8 * e + 8]
            pieces.append(jnp.concatenate([one, one], axis=0).astype(BF) * halves)
        lanes.append(jnp.concatenate(pieces, axis=0))
    full = jnp.where(same_c, nt(jnp.concatenate(lanes, axis=1), blocks_c), 0.0)
    full = full[0:16] + full[16:32] + full[32:48] + full[48:64]
    y_c = nn(jnp.concatenate([full[0:8], full[8:16]], axis=1).astype(BF), expand_c).astype(BF)

    spread_c = nn(y_c, v_tc[pl.ds(pl.multiple_of(64 * y, 64), 64), :])
    own_down = jnp.where(core == 0, spread_c[:, 0:256], spread_c[:, 256:512])
    for h in range(2):
        part = own_down[:, 128 * h : 128 * h + 128]
        part = near_b[16 * h : 16 * h + 16] + jnp.concatenate([part, part], axis=0)
        y_b = jnp.where(diagonal2[0:16], part, 0.0).astype(BF)
        spread_b = nn(y_b, v_tb[128 * h : 128 * h + 128, :])
        for j in range(2):
            for k in range(2):
                s = 4 * h + 2 * j + k
                part = spread_b[8 * j : 8 * j + 8, 256 * k : 256 * k + 256]
                part = near[32 * s : 32 * s + 32, :] + jnp.concatenate([part] * 4, axis=0)
                y_a = jnp.where(diagonal4, part, 0.0).astype(BF)
                field[32 * s : 32 * s + 32, :] = nn(y_a, v_basis[256 * s : 256 * s + 256, :]).astype(BF)

    for copy, when in sent:
        pl.when(when)(copy.wait_send)


def tiles(coupling):
    boxes = coupling.shape[0]
    split = coupling.reshape(boxes, 3, 8, 32, 128)
    return split.transpose(0, 1, 3, 2, 4).reshape(boxes, 768, 128)


def on_device(
    values,
    basis,
    transfer_b,
    transfer_c,
    coupling_a,
    lists_a,
    mask_a,
    coupling_b,
    lists_b,
    mask_b,
    coupling_c,
    lists_c,
    mask_c,
):
    groups = lax.axis_size("leaf")
    operands = (
        values.reshape(256, 256),
        basis.reshape(2048, 256),
        transfer_b.reshape(256, 512),
        transfer_c.reshape(256, 512),
        tiles(coupling_a[0]),
        tiles(coupling_b[0]),
        coupling_c[0].transpose(1, 0, 2),
        lists_a[0].T,
        mask_a[0].T,
        lists_b[0],
        mask_b[0],
        lists_c.transpose(2, 0, 1),
        mask_c.transpose(2, 0, 1),
    )
    far = pl.BlockSpec(memory_space=pltpu.HBM)
    local = pl.BlockSpec(memory_space=pltpu.VMEM)
    dma = pltpu.SemaphoreType.DMA
    field = pl.pallas_call(
        functools.partial(kernel, groups),
        out_shape=jax.ShapeDtypeStruct((256, 256), BF),
        in_specs=[far] * 13,
        out_specs=local,
        scratch_shapes=[pltpu.VMEM(x.shape, x.dtype) for x in operands]
        + [
            pltpu.VMEM((24, 128, 128), BF),
            pltpu.VMEM((24, 16, 128), BF),
            pltpu.VMEM((groups, 16, 128), BF),
            pltpu.VMEM((4, 128, 128), BF),
            pltpu.VMEM((8, 128, 128), BF),
            pltpu.VMEM((768, 768), BF),
            pltpu.VMEM((768, 512), F32),
            pltpu.VMEM((32, 128, 384), BF),
            pltpu.VMEM((32, 128, 256), BF),
            pltpu.VMEM((256, 512), BF),
            pltpu.VMEM((256, 256), F32),
        ]
        + [dma((k,)) for k in (13, 3, 3, 8, 8, 12, 12, 7, 1, 2, 2, groups - 1, 1)]
        + [pltpu.SemaphoreType.REGULAR((3,)), dma((7,)), dma((1,))],
        compiler_params=pltpu.CompilerParams(
            collective_id=0, has_side_effects=True, vmem_limit_bytes=60 * 1024 * 1024
        ),
        cost_estimate=pl.CostEstimate(flops=5_000_000_000, bytes_accessed=10_000_000, transcendentals=0),
        name="far_field",
    )(*operands)
    return field.reshape(1, 32, 8, 256)


def solution(mesh):
    in_specs = (
        P("leaf", "tel", None, None),
        P("leaf", "tel", None, None),
        P("leaf", "tel", None, None),
        P("leaf", None, None, None),
        P("leaf", "tel", None, None),
        P("leaf", "tel", None),
        P("leaf", "tel", None),
        P("leaf", "tel", None, None),
        P("leaf", "tel", None),
        P("leaf", "tel", None),
        P("leaf", None, "tel", None),
        P("leaf", None, "tel"),
        P("leaf", None, "tel"),
    )
    out_specs = P("leaf", "tel", None, None)
    return jax.shard_map(
        on_device, mesh=mesh, in_specs=in_specs, out_specs=out_specs, check_vma=False
    )
```

```python
import functools

import jax
import jax.numpy as jnp
from jax import lax
from jax.experimental import pallas as pl
from jax.experimental.pallas import tpu as pltpu
from jax.sharding import PartitionSpec as P

BF = jnp.bfloat16
F32 = jnp.float32
MESH = pl.DeviceIdType.MESH


def nt(a, b):
    return lax.dot_general(a, b, (((1,), (1,)), ((), ())), preferred_element_type=F32)


def nn(a, b):
    return jnp.dot(a, b, preferred_element_type=F32)


def grid_index(shape, dim):
    return lax.broadcasted_iota(jnp.int32, shape, dim)


def flag(condition):
    return jnp.where(condition, 1.0, 0.0)


def far_first(depth):
    offsets = [(dz, dx) for dz in range(depth) for dx in range(4) if dz or dx]
    return sorted(offsets, key=lambda o: -(min(o[0], depth - o[0]) + min(o[1], 4 - o[1])))


def column(rows, height, stride):
    sub, lane = grid_index((height, 128), 0), grid_index((height, 128), 1)
    total = jnp.zeros((height, 128), F32)
    for place, row in enumerate(rows):
        width = row.shape[1]
        wide = jnp.concatenate([row.astype(F32), jnp.zeros((1, 128 - width), F32)], axis=1)
        hit = (lane == sub - place * stride) & (lane < width)
        total = total + jnp.where(hit, jnp.broadcast_to(wide, (height, 128)), 0.0)
    return jnp.sum(total, axis=1, keepdims=True).astype(jnp.int32)


def kernel(
    groups,
    values,
    basis,
    transfer_b,
    transfer_c,
    coupling_a,
    coupling_b,
    coupling_c,
    lists_a,
    mask_a,
    lists_b,
    mask_b,
    lists_c,
    mask_c,
    out,
    v_values,
    v_basis,
    v_tb,
    v_tc,
    v_ca,
    v_cb,
    v_cc,
    v_lists_a,
    v_mask_a,
    v_lists_b,
    v_mask_b,
    v_lists_c,
    v_mask_c,
    leaf_window,
    parent_window,
    grand_window,
    share_out,
    share_in,
    pick_a,
    picked,
    left_side,
    products,
    folded,
    near,
    field,
    out_sem,
    load_sem,
    y_send,
    y_recv,
    x_send,
    x_recv,
    mate_send,
    mate_recv,
    b_send,
    b_recv,
    bx_send,
    bx_recv,
    c_send,
    c_recv,
    here,
    s_send,
    s_recv,
):
    g = lax.axis_index("leaf")
    t = lax.axis_index("tel")
    y, core = t // 2, t % 2
    depth = groups // 4

    def group_at(dz, dx):
        return lax.rem(g // 4 + dz, depth) * 4 + lax.rem(g + dx, 4)

    up, down = lax.rem(g + 1, groups), lax.rem(g + groups - 1, groups)

    loads = [
        pltpu.make_async_copy(source, target, load_sem.at[place])
        for place, (source, target) in enumerate(
            (
                (values, v_values),
                (basis, v_basis),
                (transfer_b, v_tb),
                (transfer_c, v_tc),
                (coupling_c, v_cc),
                (coupling_b, v_cb),
                (coupling_a, v_ca),
                (lists_a, v_lists_a),
                (mask_a, v_mask_a),
                (lists_b, v_lists_b),
                (mask_b, v_mask_b),
                (lists_c, v_lists_c),
                (mask_c, v_mask_c),
            )
        )
    ]
    for load in loads[0:3]:
        load.start()

    barrier = pltpu.get_barrier_semaphore()

    def greet_group(d, carry):
        pl.semaphore_signal(
            barrier, inc=1, device_id={"tel": lax.rem(t + d, 8), "leaf": g}, device_id_type=MESH
        )
        return carry

    lax.fori_loop(1, 8, greet_group, 0)
    half = groups // 2
    z, upper_half = g // 4, g >= half
    lower_half = jnp.logical_not(upper_half)

    def signal(semaphore, target):
        pl.semaphore_signal(
            semaphore, inc=1, device_id={"tel": t, "leaf": target}, device_id_type=MESH
        )

    def signal_plane(offset, along_x, when):
        @pl.when(when)
        def _():
            for dx in along_x:
                signal(barrier, (z + offset) * 4 + lax.rem(g + dx, 4))

    def signal_half(semaphore, start, when):
        def one(d, carry):
            signal(semaphore, start + lax.rem(g + d, half))
            return carry

        @pl.when(when)
        def _():
            lax.fori_loop(0, half, one, 0)

    signal_half(barrier, half, lower_half)
    signal_plane(0, (1, 2, 3), True)
    signal_plane(1, range(4), (z < depth - 1) & (z != depth // 2 - 1))
    signal_plane(-1, range(4), z > 0)

    sub, lane = grid_index((8, 128), 0), grid_index((8, 128), 1)
    left = lane < 64
    even_left = (sub % 2 == 0) & left
    odd_right = (sub % 2 == 1) & (lane >= 64)

    for end, first in ((0, 0), (groups - 1, 16)):

        @pl.when(g == end)
        def _():
            leaf_window[first : first + 8] = jnp.zeros((8, 128, 128), BF)
            parent_window[first : first + 8] = jnp.zeros((8, 16, 128), BF)

    beside = (z > 0).astype(jnp.int32) + (z < depth - 1).astype(jnp.int32)
    beside = beside - (z == depth // 2).astype(jnp.int32)
    pl.semaphore_wait(barrier, 10 + 4 * beside + half * upper_half.astype(jnp.int32))
    signal_half(here.at[0], 0, upper_half)
    pl.when(upper_half & (z < depth - 1))(lambda: signal(here.at[1], g + 4))
    pl.when(upper_half & (z > depth // 2))(lambda: signal(here.at[1], g - 4))
    loads[0].wait()
    loads[1].wait()
    for load in loads[7:13] + loads[3:7]:
        load.start()
    placed, stacked = [], []
    for s in range(8):
        product = nt(v_values[32 * s : 32 * s + 32, :], v_basis[256 * s : 256 * s + 256, :])
        for h in range(2):
            first = product[16 * h : 16 * h + 8, 128 * h : 128 * h + 128]
            second = product[16 * h + 8 : 16 * h + 16, 128 * h : 128 * h + 128]
            placed.append(
                jnp.where(even_left, first, jnp.where(odd_right, pltpu.roll(first, 64, 1), 0.0))
            )
            placed.append(
                jnp.where(even_left, pltpu.roll(second, 64, 1), jnp.where(odd_right, second, 0.0))
            )
            stacked.append(jnp.where(left, first, second))
    placed = jnp.concatenate(placed, axis=0).astype(BF)
    row = grid_index((128, 1), 0)
    first = (row % 32) * 8 + (row // 32) * 2
    order = flag(jnp.broadcast_to(first, (128, 256)) == (grid_index((128, 256), 1) & -2)).astype(BF)
    own_slot = 8 + core * 4 + y
    leaf_window[own_slot] = nn(order, placed).astype(BF)

    loads[2].wait()
    lifted = []
    for b in range(4):
        children = jnp.concatenate(stacked[4 * b : 4 * b + 4], axis=1).astype(BF)
        lifted.append(nt(children, v_tb[64 * b : 64 * b + 64, :]))
    parent_window[8 + t] = jnp.concatenate(
        [jnp.concatenate(lifted[0:2], axis=1), jnp.concatenate(lifted[2:4], axis=1)], axis=0
    ).astype(BF)

    def send(source, target, send_sem, recv_sem, tel, leaf, when=True):
        copy = pltpu.make_async_remote_copy(
            src_ref=source,
            dst_ref=target,
            send_sem=send_sem,
            recv_sem=recv_sem,
            device_id={"tel": tel, "leaf": leaf},
            device_id_type=MESH,
        )
        pl.when(when)(copy.start)
        return copy, when

    sent = []
    for d in range(1, 8):
        block = parent_window.at[8 + t]
        sent.append(send(block, block, b_send.at[d - 1], b_recv.at[0], lax.rem(t + d, 8), g))

    mate = t + 1 - 2 * core

    has_up, has_down = g < groups - 1, g > 0

    def spread(slot, place):
        block = leaf_window.at[slot]
        sent.append(
            send(block, leaf_window.at[slot - 8], x_send.at[place], x_recv.at[place], t, up, has_up)
        )
        sent.append(
            send(
                block, leaf_window.at[slot + 8], x_send.at[4 + place], x_recv.at[4 + place], t, down, has_down
            )
        )
        sent.append(send(block, block, mate_send.at[place], mate_recv.at[place], mate, g))

    own = leaf_window.at[own_slot]
    for d in range(1, 4):
        sent.append(
            send(own, own, y_send.at[d - 1], y_recv.at[d - 1], lax.rem(y + d, 4) * 2 + core, g)
        )
    spread(own_slot, 0)

    @pl.when(upper_half)
    def _():
        pl.semaphore_wait(here.at[1], 1 + ((z > depth // 2) & (z < depth - 1)).astype(jnp.int32))
        signal(here.at[2], jnp.where(z < depth // 2 + 2, g + 8, g - 8))

    def received(ref, sem, when=True):
        pl.when(when)(pltpu.make_async_copy(ref, ref, sem).wait)

    loads[7].wait()
    loads[8].wait()
    local = v_lists_a[...] - (g - 1) * 256
    inner = local % 256
    slot = (local // 256) * 8 + ((inner // 32) % 2) * 4 + inner // 64
    place = jnp.where(v_mask_a[...] == 1, slot * 32 + inner % 32, -1)
    lane24 = grid_index((24, 128), 1)
    for pair in range(16):
        rows = []
        for n in (2 * pair, 2 * pair + 1):
            wide = jnp.broadcast_to(place[:, n : n + 1], (24, 128)) - lane24
            rows.append(jnp.concatenate([flag(wide == 128 * k) for k in range(6)], axis=1))
        pick_a[48 * pair : 48 * pair + 48, :] = jnp.concatenate(rows, axis=0).astype(BF)

    for d in range(1, 4):
        source = 8 + core * 4 + lax.rem(y + 4 - d, 4)
        received(leaf_window.at[source], y_recv.at[d - 1])
        spread(source, d)

    received(parent_window.at[pl.ds(0, 7)], b_recv.at[0])
    loads[3].wait()
    lifted = []
    for c in range(4):
        one = parent_window[8 + 2 * c].astype(F32)
        two = parent_window[9 + 2 * c].astype(F32)
        children = jnp.concatenate([one[0:8], one[8:16], two[0:8], two[8:16]], axis=1).astype(BF)
        lifted.append(nt(children, v_tc[64 * c : 64 * c + 64, :]))
    grand_window[g] = jnp.concatenate(
        [jnp.concatenate(lifted[0:2], axis=1), jnp.concatenate(lifted[2:4], axis=1)], axis=0
    ).astype(BF)

    block = grand_window.at[g]
    grand_copies = [
        pltpu.make_async_remote_copy(
            src_ref=block,
            dst_ref=block,
            send_sem=c_send.at[k],
            recv_sem=c_recv.at[0],
            device_id={"tel": t, "leaf": group_at(dz, dx)},
            device_id_type=MESH,
        )
        for k, (dz, dx) in enumerate(far_first(depth))
    ]
    sent.extend((copy, True) for copy in grand_copies)

    def send_grand(semaphore, count):
        pl.semaphore_wait(semaphore, count)
        for copy in grand_copies:
            copy.start()

    pl.when(upper_half)(lambda: send_grand(here.at[2], 1))

    group_parents = parent_window.at[pl.ds(8, 8)]
    sent.append(
        send(group_parents, parent_window.at[pl.ds(0, 8)], bx_send.at[0], bx_recv.at[0], t, up, has_up)
    )
    sent.append(
        send(group_parents, parent_window.at[pl.ds(16, 8)], bx_send.at[1], bx_recv.at[1], t, down, has_down)
    )

    loads[4].wait()
    for load in loads[9:13]:
        load.wait()
    codes = jnp.zeros((4, 128), F32)
    lane4 = grid_index((4, 128), 1)
    for p in range(3):
        entry = column([v_lists_c[p]], 4, 0)
        valid = column([v_mask_c[p]], 4, 0)
        code = jnp.where(valid == 1, entry, -1).astype(F32)
        codes = jnp.where(lane4 == p, jnp.broadcast_to(code, (4, 128)), codes)
    codes = jnp.concatenate([codes, jnp.zeros((4, 4096 - 128), F32)], axis=1)
    upper = jnp.concatenate([v_cc[0].astype(F32), v_cc[1].astype(F32)], axis=0)
    lower = jnp.concatenate([v_cc[2].astype(F32), codes], axis=0)
    blocks_c = []
    for k in range(32):
        blocks_c.append(upper[:, 128 * k : 128 * k + 128])
        blocks_c.append(lower[:, 128 * k : 128 * k + 128])
    blocks_c = jnp.concatenate(blocks_c, axis=0).astype(BF)
    row = grid_index((512, 1), 0)
    source = ((row % 128) // 4) * 16 + (row % 4) * 4 + row // 128
    regroup = flag(jnp.broadcast_to(source, (512, 512)) == grid_index((512, 512), 1))
    blocks_c = nn(regroup.astype(BF), blocks_c).astype(BF)
    for c in range(4):
        share_out[c] = blocks_c[128 * c : 128 * c + 128]
    share_in[core * 4 + y] = share_out[y]
    for d in range(1, 4):
        owner = lax.rem(y + d, 4)
        sent.append(
            send(
                share_out.at[owner],
                share_in.at[core * 4 + y],
                s_send.at[d - 1],
                s_recv.at[0],
                owner * 2 + core,
                g,
            )
        )

    choose_b, half_b = [], []
    lane384 = grid_index((8, 384), 1)
    for n in range(4):
        entry = column([v_lists_b[n : n + 1, :]], 24, 0) - (g - 1) * 32
        valid = column([v_mask_b[n : n + 1, :]], 24, 0)
        base = jnp.where(valid == 1, (entry // 2) * 8, -1000)
        for i in range(3):
            wide = jnp.broadcast_to(base[8 * i : 8 * i + 8], (8, 384)) - lane384
            choose_b.extend(flag(wide == -r) for r in range(8))
            half_b.append(jnp.broadcast_to(entry[8 * i : 8 * i + 8] % 2, (8, 128)) == lane // 64)
    choose_b = jnp.concatenate(choose_b, axis=0).astype(BF)

    pl.when(lower_half)(lambda: send_grand(here.at[0], half))
    received(share_in.at[pl.ds(0, 3)], s_recv.at[0])
    shares = share_in.at[pl.ds(core * 4, 4)]
    sent.append(send(shares, shares, s_send.at[3], s_recv.at[1], mate, g))

    for d in range(4):
        source = core * 4 + lax.rem(y + 4 - d, 4)
        for side in range(2):
            block = leaf_window.at[source + 16 * side]
            there = (has_down, has_up)[side]
            received(block, x_recv.at[4 * side + d], there)
            k = 4 + 2 * d + side
            sent.append(send(block, block, mate_send.at[k], mate_recv.at[k], mate, g, there))


    row, col = grid_index((128, 256), 0), grid_index((128, 256), 1)
    same_p = row % 8 == col % 8
    row, col = grid_index((32, 256), 0), grid_index((32, 256), 1)
    fold = flag(
        ((row // 8) % 2 == col // 128) & (row % 8 == (col // 16) % 8) & (row // 16 == (col // 8) % 2)
    ).astype(BF)
    diagonal4 = row // 8 == col // 64
    row = grid_index((512, 1), 0)
    target = 2 * ((row % 256) // 8) + row // 256
    expand = flag(jnp.broadcast_to(target, (512, 128)) == grid_index((512, 128), 1) % 64).astype(BF)
    expand = jnp.concatenate([expand, expand], axis=1)
    row, col = grid_index((32, 128), 0), grid_index((32, 128), 1)
    diagonal2 = (row // 8) % 2 == col // 64
    row, col = grid_index((16, 128), 0), grid_index((16, 128), 1)
    halves = flag(row // 8 == col // 64).astype(BF)

    def couple(lhs, coupling):
        wide = jnp.concatenate([coupling[256 * i : 256 * i + 256] for i in range(3)], axis=1)
        return jnp.where(same_p, nt(lhs, wide), 0.0).astype(BF)

    def fold_pair(pair):
        both = nn(fold, pair)
        return jnp.concatenate([both[0:16], both[16:32]], axis=1).astype(BF)

    received(parent_window.at[pl.ds(0, 8)], bx_recv.at[0], has_down)
    received(parent_window.at[pl.ds(16, 8)], bx_recv.at[1], has_up)
    loads[5].wait()
    found = nn(choose_b, parent_window[...].reshape(384, 128))
    rows, pair = [], []
    for n in range(4):
        lanes = []
        for i in range(3):
            pieces = []
            for r in range(8):
                at = 8 * ((n * 3 + i) * 8 + r)
                one = found[at : at + 8]
                both = jnp.where(half_b[n * 3 + i], one, pltpu.roll(one, 64, 1))
                pieces.append(jnp.concatenate([both, both], axis=0).astype(BF) * halves)
            lanes.append(jnp.concatenate(pieces, axis=0))
        pair.append(couple(jnp.concatenate(lanes, axis=1), v_cb[n]))
        if n % 2:
            rows.append(fold_pair(jnp.concatenate(pair, axis=0)))
            pair = []
    near_b = nn(jnp.concatenate(rows, axis=0), expand[:, 0:128])


    for k in range(4):
        if k == 0:
            block = leaf_window.at[8 + (1 - core) * 4 + y]
        else:
            block = leaf_window.at[8 + (1 - core) * 4 + lax.rem(y + 4 - k, 4)]
        received(block, mate_recv.at[k])
    for d in range(4):
        source = (1 - core) * 4 + lax.rem(y + 4 - d, 4)
        for side in range(2):
            received(
                leaf_window.at[source + 16 * side], mate_recv.at[4 + 2 * d + side], (has_down, has_up)[side]
            )
    loads[6].wait()
    for half in range(2):
        window = jnp.concatenate(
            [
                leaf_window[:, 32 * k : 32 * k + 32, :].reshape(768, 128)
                for k in (2 * half, 2 * half + 1)
            ],
            axis=1,
        )
        picked[:, 256 * half : 256 * half + 256] = nn(pick_a[...], window)

    def build(n, carry):
        lanes = []
        for i in range(3):
            eight = picked[pl.ds(pl.multiple_of(24 * n + 8 * i, 8), 8), :]
            pieces = []
            for k in range(4):
                one = eight[:, 128 * k : 128 * k + 128]
                turned = pltpu.roll(one, 64, 1)
                pieces.append(jnp.concatenate([one, turned], axis=0).astype(BF) * halves)
                pieces.append(jnp.concatenate([turned, one], axis=0).astype(BF) * halves)
            lanes.append(jnp.concatenate(pieces, axis=0))
        left_side[n] = jnp.concatenate(lanes, axis=1)
        return carry

    def multiply(n, carry):
        products[n] = couple(left_side[n], v_ca.at[n])
        return carry

    def fold_products(pair, carry):
        rows = products[pl.ds(2 * pair, 2)].reshape(256, 256)
        folded[pl.ds(pl.multiple_of(16 * pair, 16), 16), :] = fold_pair(rows)
        return carry

    lax.fori_loop(0, 32, build, 0, unroll=32)
    lax.fori_loop(0, 32, multiply, 0, unroll=32)
    lax.fori_loop(0, 16, fold_products, 0, unroll=16)
    near_a = nn(folded[...], expand)
    for h in range(2):
        y_b = jnp.where(diagonal2[0:16], near_b[16 * h : 16 * h + 16], 0.0).astype(BF)
        spread_b = nn(y_b, v_tb[128 * h : 128 * h + 128, :])
        for j in range(2):
            for k in range(2):
                s = 4 * h + 2 * j + k
                part = spread_b[8 * j : 8 * j + 8, 256 * k : 256 * k + 256]
                near[32 * s : 32 * s + 32, :] = near_a[32 * s : 32 * s + 32] + jnp.concatenate([part] * 4, axis=0)

    own_c = v_tc[pl.ds(pl.multiple_of(64 * y, 64), 64), :]
    own_c = jnp.where(core == 0, own_c[:, 0:256].astype(F32), own_c[:, 256:512].astype(F32)).astype(BF)
    down_c = jnp.concatenate(
        [nn(own_c[:, 64 * b : 64 * b + 64], v_tb[64 * b : 64 * b + 64, :]) for b in range(4)], axis=1
    ).astype(BF)

    received(share_in.at[pl.ds(0, 4)], s_recv.at[1])
    grand_rows = 16 * groups
    row, lane32 = grid_index((32, 128), 0), grid_index((32, 128), 1)
    choose_c, half_c = [], []
    for source in range(8):
        code = jnp.broadcast_to(share_in[source, 0:16, :].astype(F32)[3:4], (32, 128))
        code = jnp.sum(jnp.where(lane32 == row // 8, code, 0.0), axis=1, keepdims=True).astype(jnp.int32)
        row1 = grid_index((32, 1), 0)
        base = jnp.where((code >= 0) & (row1 < 24), (code // 2) * 8 + row1 % 8, -1000)
        hit = jnp.broadcast_to(base, (32, grand_rows)) == grid_index((32, grand_rows), 1)
        choose_c.append(flag(hit))
        half_c.append(jnp.broadcast_to(code % 2, (32, 128)) == lane32 // 64)
    choose_c = jnp.concatenate(choose_c, axis=0).astype(BF)
    half_c = jnp.concatenate(half_c, axis=0)
    blocks_c = jnp.concatenate([share_in[source] for source in range(8)], axis=1)
    row, col = grid_index((64, 128), 0), grid_index((64, 128), 1)
    same_c = row // 16 == col % 4
    row, col = grid_index((256, 64), 0), grid_index((256, 64), 1)
    expand_c = flag(col == 2 * ((row % 128) // 4) + row // 128).astype(BF)

    received(grand_window.at[pl.ds(0, groups - 1)], c_recv.at[0])
    found = nn(choose_c, grand_window[...].reshape(grand_rows, 128))
    found = jnp.where(half_c, found, pltpu.roll(found, 64, 1))
    lanes = []
    for source in range(8):
        pieces = []
        for e in range(4):
            one = found[32 * source + 8 * e : 32 * source + 8 * e + 8]
            pieces.append(jnp.concatenate([one, one], axis=0).astype(BF) * halves)
        lanes.append(jnp.concatenate(pieces, axis=0))
    full = jnp.where(same_c, nt(jnp.concatenate(lanes, axis=1), blocks_c), 0.0)
    full = full[0:16] + full[16:32] + full[32:48] + full[48:64]
    y_c = nn(jnp.concatenate([full[0:8], full[8:16]], axis=1).astype(BF), expand_c).astype(BF)

    from_c = nn(y_c, down_c)
    writes = []
    for s in range(8):
        part = from_c[:, 256 * s : 256 * s + 256]
        part = near[32 * s : 32 * s + 32, :] + jnp.concatenate([part] * 4, axis=0)
        y_a = jnp.where(diagonal4, part, 0.0).astype(BF)
        rows = pl.ds(32 * s, 32)
        field[rows, :] = nn(y_a, v_basis[256 * s : 256 * s + 256, :]).astype(BF)
        writes.append(pltpu.make_async_copy(field.at[rows], out.at[rows], out_sem.at[s]))
        writes[-1].start()

    for copy, when in sent:
        pl.when(when)(copy.wait_send)
    for write in writes:
        write.wait()


def tiles(coupling):
    boxes = coupling.shape[0]
    split = coupling.reshape(boxes, 3, 8, 32, 128)
    return split.transpose(0, 1, 3, 2, 4).reshape(boxes, 768, 128)


def on_device(
    values,
    basis,
    transfer_b,
    transfer_c,
    coupling_a,
    lists_a,
    mask_a,
    coupling_b,
    lists_b,
    mask_b,
    coupling_c,
    lists_c,
    mask_c,
):
    groups = lax.axis_size("leaf")
    operands = (
        values.reshape(256, 256),
        basis.reshape(2048, 256),
        transfer_b.reshape(256, 512),
        transfer_c.reshape(256, 512),
        tiles(coupling_a[0]),
        tiles(coupling_b[0]),
        coupling_c[0].transpose(1, 0, 2),
        lists_a[0].T,
        mask_a[0].T,
        lists_b[0],
        mask_b[0],
        lists_c.transpose(2, 0, 1),
        mask_c.transpose(2, 0, 1),
    )
    far = pl.BlockSpec(memory_space=pltpu.HBM)
    dma = pltpu.SemaphoreType.DMA
    field = pl.pallas_call(
        functools.partial(kernel, groups),
        out_shape=jax.ShapeDtypeStruct((256, 256), BF),
        in_specs=[far] * 13,
        out_specs=far,
        scratch_shapes=[pltpu.VMEM(x.shape, x.dtype) for x in operands]
        + [
            pltpu.VMEM((24, 128, 128), BF),
            pltpu.VMEM((24, 16, 128), BF),
            pltpu.VMEM((groups, 16, 128), BF),
            pltpu.VMEM((4, 128, 128), BF),
            pltpu.VMEM((8, 128, 128), BF),
            pltpu.VMEM((768, 768), BF),
            pltpu.VMEM((768, 512), F32),
            pltpu.VMEM((32, 128, 384), BF),
            pltpu.VMEM((32, 128, 256), BF),
            pltpu.VMEM((256, 512), BF),
            pltpu.VMEM((256, 256), F32),
            pltpu.VMEM((256, 256), BF),
            dma((8,)),
        ]
        + [dma((k,)) for k in (13, 3, 3, 8, 8, 12, 12, 7, 1, 2, 2, groups - 1, 1)]
        + [pltpu.SemaphoreType.REGULAR((3,)), dma((4,)), dma((2,))],
        compiler_params=pltpu.CompilerParams(
            collective_id=0, has_side_effects=True, vmem_limit_bytes=60 * 1024 * 1024
        ),
        cost_estimate=pl.CostEstimate(flops=5_000_000_000, bytes_accessed=10_000_000, transcendentals=0),
        name="far_field",
    )(*operands)
    return field.reshape(1, 32, 8, 256)


def solution(mesh):
    in_specs = (
        P("leaf", "tel", None, None),
        P("leaf", "tel", None, None),
        P("leaf", "tel", None, None),
        P("leaf", None, None, None),
        P("leaf", "tel", None, None),
        P("leaf", "tel", None),
        P("leaf", "tel", None),
        P("leaf", "tel", None, None),
        P("leaf", "tel", None),
        P("leaf", "tel", None),
        P("leaf", None, "tel", None),
        P("leaf", None, "tel"),
        P("leaf", None, "tel"),
    )
    out_specs = P("leaf", "tel", None, None)
    return jax.shard_map(
        on_device, mesh=mesh, in_specs=in_specs, out_specs=out_specs, check_vma=False
    )
```

```python
import functools

import jax
import jax.numpy as jnp
from jax import lax
from jax.experimental import pallas as pl
from jax.experimental.pallas import tpu as pltpu
from jax.sharding import PartitionSpec as P

BF = jnp.bfloat16
F32 = jnp.float32
MESH = pl.DeviceIdType.MESH


def nt(a, b):
    return lax.dot_general(a, b, (((1,), (1,)), ((), ())), preferred_element_type=F32)


def nn(a, b):
    return jnp.dot(a, b, preferred_element_type=F32)


def grid_index(shape, dim):
    return lax.broadcasted_iota(jnp.int32, shape, dim)


def flag(condition):
    return jnp.where(condition, 1.0, 0.0)


def far_first(depth):
    offsets = [(dz, dx) for dz in range(depth) for dx in range(4) if dz or dx]
    return sorted(offsets, key=lambda o: -(min(o[0], depth - o[0]) + min(o[1], 4 - o[1])))


def column(rows, height, stride):
    sub, lane = grid_index((height, 128), 0), grid_index((height, 128), 1)
    total = jnp.zeros((height, 128), F32)
    for place, row in enumerate(rows):
        width = row.shape[1]
        wide = jnp.concatenate([row.astype(F32), jnp.zeros((1, 128 - width), F32)], axis=1)
        hit = (lane == sub - place * stride) & (lane < width)
        total = total + jnp.where(hit, jnp.broadcast_to(wide, (height, 128)), 0.0)
    return jnp.sum(total, axis=1, keepdims=True).astype(jnp.int32)


def kernel(
    groups,
    values,
    basis,
    transfer_b,
    transfer_c,
    coupling_a,
    coupling_b,
    coupling_c,
    lists_a,
    mask_a,
    lists_b,
    mask_b,
    lists_c,
    mask_c,
    out,
    v_values,
    v_basis,
    v_tb,
    v_tc,
    v_ca,
    v_cb,
    v_cc,
    v_lists_a,
    v_mask_a,
    v_lists_b,
    v_mask_b,
    v_lists_c,
    v_mask_c,
    leaf_window,
    parent_window,
    grand_window,
    share_out,
    share_in,
    pick_a,
    picked,
    left_side,
    products,
    folded,
    near,
    field,
    out_sem,
    load_sem,
    y_send,
    y_recv,
    x_send,
    x_recv,
    mate_send,
    mate_recv,
    b_send,
    b_recv,
    bx_send,
    bx_recv,
    c_send,
    c_recv,
    here,
    s_send,
    s_recv,
):
    g = lax.axis_index("leaf")
    t = lax.axis_index("tel")
    y, core = t // 2, t % 2
    depth = groups // 4

    def group_at(dz, dx):
        return lax.rem(g // 4 + dz, depth) * 4 + lax.rem(g + dx, 4)

    up, down = lax.rem(g + 1, groups), lax.rem(g + groups - 1, groups)

    loads = [
        pltpu.make_async_copy(source, target, load_sem.at[place])
        for place, (source, target) in enumerate(
            (
                (values, v_values),
                (basis, v_basis),
                (transfer_b, v_tb),
                (transfer_c, v_tc),
                (coupling_c, v_cc),
                (coupling_b, v_cb),
                (coupling_a, v_ca),
                (lists_a, v_lists_a),
                (mask_a, v_mask_a),
                (lists_b, v_lists_b),
                (mask_b, v_mask_b),
                (lists_c, v_lists_c),
                (mask_c, v_mask_c),
            )
        )
    ]
    for load in loads[0:3]:
        load.start()

    barrier = pltpu.get_barrier_semaphore()

    def greet_group(d, carry):
        pl.semaphore_signal(
            barrier, inc=1, device_id={"tel": lax.rem(t + d, 8), "leaf": g}, device_id_type=MESH
        )
        return carry

    lax.fori_loop(1, 8, greet_group, 0)
    half = groups // 2
    z, upper_half = g // 4, g >= half
    lower_half = jnp.logical_not(upper_half)

    def signal(semaphore, target):
        pl.semaphore_signal(
            semaphore, inc=1, device_id={"tel": t, "leaf": target}, device_id_type=MESH
        )

    def signal_plane(offset, along_x, when):
        @pl.when(when)
        def _():
            for dx in along_x:
                signal(barrier, (z + offset) * 4 + lax.rem(g + dx, 4))

    def signal_half(semaphore, start, when):
        def one(d, carry):
            signal(semaphore, start + lax.rem(g + d, half))
            return carry

        @pl.when(when)
        def _():
            lax.fori_loop(0, half, one, 0)

    signal_half(barrier, half, lower_half)
    signal_plane(0, (1, 2, 3), True)
    signal_plane(1, range(4), upper_half & (z < depth - 1))
    signal_plane(-1, range(4), z > depth // 2)
    first_x, last_x = g % 4 == 0, g % 4 == 3
    pl.when(lower_half & last_x & (z < depth // 2 - 1))(lambda: signal(barrier, g + 1))
    pl.when(first_x & (z > 0) & (z <= depth // 2))(lambda: signal(barrier, g - 1))

    sub, lane = grid_index((8, 128), 0), grid_index((8, 128), 1)
    left = lane < 64
    even_left = (sub % 2 == 0) & left
    odd_right = (sub % 2 == 1) & (lane >= 64)

    for end, first in ((0, 0), (groups - 1, 16)):

        @pl.when(g == end)
        def _():
            leaf_window[first : first + 8] = jnp.zeros((8, 128, 128), BF)
            parent_window[first : first + 8] = jnp.zeros((8, 16, 128), BF)

    beside = (z > depth // 2).astype(jnp.int32) + (z < depth - 1).astype(jnp.int32)
    pl.when(upper_half)(lambda: pl.semaphore_wait(barrier, 10 + 4 * beside + half))
    signal_half(here.at[0], 0, upper_half)
    pl.when(upper_half & (z < depth - 1))(lambda: signal(here.at[1], g + 4))
    pl.when(upper_half & (z > depth // 2))(lambda: signal(here.at[1], g - 4))
    loads[0].wait()
    loads[1].wait()
    for load in loads[7:13] + loads[3:7]:
        load.start()
    placed, stacked = [], []
    for s in range(8):
        product = nt(v_values[32 * s : 32 * s + 32, :], v_basis[256 * s : 256 * s + 256, :])
        for h in range(2):
            first = product[16 * h : 16 * h + 8, 128 * h : 128 * h + 128]
            second = product[16 * h + 8 : 16 * h + 16, 128 * h : 128 * h + 128]
            placed.append(
                jnp.where(even_left, first, jnp.where(odd_right, pltpu.roll(first, 64, 1), 0.0))
            )
            placed.append(
                jnp.where(even_left, pltpu.roll(second, 64, 1), jnp.where(odd_right, second, 0.0))
            )
            stacked.append(jnp.where(left, first, second))
    placed = jnp.concatenate(placed, axis=0).astype(BF)
    row = grid_index((128, 1), 0)
    first = (row % 32) * 8 + (row // 32) * 2
    order = flag(jnp.broadcast_to(first, (128, 256)) == (grid_index((128, 256), 1) & -2)).astype(BF)
    own_slot = 8 + core * 4 + y
    leaf_window[own_slot] = nn(order, placed).astype(BF)

    loads[2].wait()
    lifted = []
    for b in range(4):
        children = jnp.concatenate(stacked[4 * b : 4 * b + 4], axis=1).astype(BF)
        lifted.append(nt(children, v_tb[64 * b : 64 * b + 64, :]))
    parent_window[8 + t] = jnp.concatenate(
        [jnp.concatenate(lifted[0:2], axis=1), jnp.concatenate(lifted[2:4], axis=1)], axis=0
    ).astype(BF)

    def send(source, target, send_sem, recv_sem, tel, leaf, when=True):
        copy = pltpu.make_async_remote_copy(
            src_ref=source,
            dst_ref=target,
            send_sem=send_sem,
            recv_sem=recv_sem,
            device_id={"tel": tel, "leaf": leaf},
            device_id_type=MESH,
        )
        pl.when(when)(copy.start)
        return copy, when

    ends = last_x.astype(jnp.int32) + (first_x & (z > 0)).astype(jnp.int32)
    pl.when(lower_half)(lambda: pl.semaphore_wait(barrier, 10 + ends))

    sent = []
    for d in range(1, 8):
        block = parent_window.at[8 + t]
        sent.append(send(block, block, b_send.at[d - 1], b_recv.at[0], lax.rem(t + d, 8), g))

    mate = t + 1 - 2 * core

    has_up, has_down = g < groups - 1, g > 0

    def spread(slot, place):
        block = leaf_window.at[slot]
        sent.append(
            send(block, leaf_window.at[slot - 8], x_send.at[place], x_recv.at[place], t, up, has_up)
        )
        sent.append(
            send(
                block, leaf_window.at[slot + 8], x_send.at[4 + place], x_recv.at[4 + place], t, down, has_down
            )
        )
        sent.append(send(block, block, mate_send.at[place], mate_recv.at[place], mate, g))

    own = leaf_window.at[own_slot]
    for d in range(1, 4):
        sent.append(
            send(own, own, y_send.at[d - 1], y_recv.at[d - 1], lax.rem(y + d, 4) * 2 + core, g)
        )
    spread(own_slot, 0)

    @pl.when(upper_half)
    def _():
        pl.semaphore_wait(here.at[1], 1 + ((z > depth // 2) & (z < depth - 1)).astype(jnp.int32))
        signal(here.at[2], jnp.where(z < depth // 2 + 2, g + 8, g - 8))

    def received(ref, sem, when=True):
        pl.when(when)(pltpu.make_async_copy(ref, ref, sem).wait)

    loads[7].wait()
    loads[8].wait()
    local = v_lists_a[...] - (g - 1) * 256
    inner = local % 256
    slot = (local // 256) * 8 + ((inner // 32) % 2) * 4 + inner // 64
    place = jnp.where(v_mask_a[...] == 1, slot * 32 + inner % 32, -1)
    lane24 = grid_index((24, 128), 1)
    for pair in range(16):
        rows = []
        for n in (2 * pair, 2 * pair + 1):
            wide = jnp.broadcast_to(place[:, n : n + 1], (24, 128)) - lane24
            rows.append(jnp.concatenate([flag(wide == 128 * k) for k in range(6)], axis=1))
        pick_a[48 * pair : 48 * pair + 48, :] = jnp.concatenate(rows, axis=0).astype(BF)

    for d in range(1, 4):
        source = 8 + core * 4 + lax.rem(y + 4 - d, 4)
        received(leaf_window.at[source], y_recv.at[d - 1])
        spread(source, d)

    received(parent_window.at[pl.ds(0, 7)], b_recv.at[0])
    loads[3].wait()
    lifted = []
    for c in range(4):
        one = parent_window[8 + 2 * c].astype(F32)
        two = parent_window[9 + 2 * c].astype(F32)
        children = jnp.concatenate([one[0:8], one[8:16], two[0:8], two[8:16]], axis=1).astype(BF)
        lifted.append(nt(children, v_tc[64 * c : 64 * c + 64, :]))
    grand_window[g] = jnp.concatenate(
        [jnp.concatenate(lifted[0:2], axis=1), jnp.concatenate(lifted[2:4], axis=1)], axis=0
    ).astype(BF)

    block = grand_window.at[g]
    grand_copies = [
        pltpu.make_async_remote_copy(
            src_ref=block,
            dst_ref=block,
            send_sem=c_send.at[k],
            recv_sem=c_recv.at[0],
            device_id={"tel": t, "leaf": group_at(dz, dx)},
            device_id_type=MESH,
        )
        for k, (dz, dx) in enumerate(far_first(depth))
    ]
    sent.extend((copy, True) for copy in grand_copies)

    def send_grand(semaphore, count):
        pl.semaphore_wait(semaphore, count)
        for copy in grand_copies:
            copy.start()

    pl.when(upper_half)(lambda: send_grand(here.at[2], 1))

    group_parents = parent_window.at[pl.ds(8, 8)]
    sent.append(
        send(group_parents, parent_window.at[pl.ds(0, 8)], bx_send.at[0], bx_recv.at[0], t, up, has_up)
    )
    sent.append(
        send(group_parents, parent_window.at[pl.ds(16, 8)], bx_send.at[1], bx_recv.at[1], t, down, has_down)
    )

    loads[4].wait()
    for load in loads[9:13]:
        load.wait()
    codes = jnp.zeros((4, 128), F32)
    lane4 = grid_index((4, 128), 1)
    for p in range(3):
        entry = column([v_lists_c[p]], 4, 0)
        valid = column([v_mask_c[p]], 4, 0)
        code = jnp.where(valid == 1, entry, -1).astype(F32)
        codes = jnp.where(lane4 == p, jnp.broadcast_to(code, (4, 128)), codes)
    codes = jnp.concatenate([codes, jnp.zeros((4, 4096 - 128), F32)], axis=1)
    upper = jnp.concatenate([v_cc[0].astype(F32), v_cc[1].astype(F32)], axis=0)
    lower = jnp.concatenate([v_cc[2].astype(F32), codes], axis=0)
    blocks_c = []
    for k in range(32):
        blocks_c.append(upper[:, 128 * k : 128 * k + 128])
        blocks_c.append(lower[:, 128 * k : 128 * k + 128])
    blocks_c = jnp.concatenate(blocks_c, axis=0).astype(BF)
    row = grid_index((512, 1), 0)
    source = ((row % 128) // 4) * 16 + (row % 4) * 4 + row // 128
    regroup = flag(jnp.broadcast_to(source, (512, 512)) == grid_index((512, 512), 1))
    blocks_c = nn(regroup.astype(BF), blocks_c).astype(BF)
    for c in range(4):
        share_out[c] = blocks_c[128 * c : 128 * c + 128]
    share_in[core * 4 + y] = share_out[y]
    for d in range(1, 4):
        owner = lax.rem(y + d, 4)
        sent.append(
            send(
                share_out.at[owner],
                share_in.at[core * 4 + y],
                s_send.at[d - 1],
                s_recv.at[0],
                owner * 2 + core,
                g,
            )
        )

    choose_b, half_b = [], []
    lane384 = grid_index((8, 384), 1)
    for n in range(4):
        entry = column([v_lists_b[n : n + 1, :]], 24, 0) - (g - 1) * 32
        valid = column([v_mask_b[n : n + 1, :]], 24, 0)
        base = jnp.where(valid == 1, (entry // 2) * 8, -1000)
        for i in range(3):
            wide = jnp.broadcast_to(base[8 * i : 8 * i + 8], (8, 384)) - lane384
            choose_b.extend(flag(wide == -r) for r in range(8))
            half_b.append(jnp.broadcast_to(entry[8 * i : 8 * i + 8] % 2, (8, 128)) == lane // 64)
    choose_b = jnp.concatenate(choose_b, axis=0).astype(BF)

    pl.when(lower_half)(lambda: send_grand(here.at[0], half))
    received(share_in.at[pl.ds(0, 3)], s_recv.at[0])
    shares = share_in.at[pl.ds(core * 4, 4)]
    sent.append(send(shares, shares, s_send.at[3], s_recv.at[1], mate, g))

    for d in range(4):
        source = core * 4 + lax.rem(y + 4 - d, 4)
        for side in range(2):
            block = leaf_window.at[source + 16 * side]
            there = (has_down, has_up)[side]
            received(block, x_recv.at[4 * side + d], there)
            k = 4 + 2 * d + side
            sent.append(send(block, block, mate_send.at[k], mate_recv.at[k], mate, g, there))


    row, col = grid_index((128, 256), 0), grid_index((128, 256), 1)
    same_p = row % 8 == col % 8
    row, col = grid_index((32, 256), 0), grid_index((32, 256), 1)
    fold = flag(
        ((row // 8) % 2 == col // 128) & (row % 8 == (col // 16) % 8) & (row // 16 == (col // 8) % 2)
    ).astype(BF)
    diagonal4 = row // 8 == col // 64
    row = grid_index((512, 1), 0)
    target = 2 * ((row % 256) // 8) + row // 256
    expand = flag(jnp.broadcast_to(target, (512, 128)) == grid_index((512, 128), 1) % 64).astype(BF)
    expand = jnp.concatenate([expand, expand], axis=1)
    row, col = grid_index((32, 128), 0), grid_index((32, 128), 1)
    diagonal2 = (row // 8) % 2 == col // 64
    row, col = grid_index((16, 128), 0), grid_index((16, 128), 1)
    halves = flag(row // 8 == col // 64).astype(BF)

    def couple(lhs, coupling):
        wide = jnp.concatenate([coupling[256 * i : 256 * i + 256] for i in range(3)], axis=1)
        return jnp.where(same_p, nt(lhs, wide), 0.0).astype(BF)

    def fold_pair(pair):
        both = nn(fold, pair)
        return jnp.concatenate([both[0:16], both[16:32]], axis=1).astype(BF)

    received(parent_window.at[pl.ds(0, 8)], bx_recv.at[0], has_down)
    received(parent_window.at[pl.ds(16, 8)], bx_recv.at[1], has_up)
    loads[5].wait()
    found = nn(choose_b, parent_window[...].reshape(384, 128))
    rows, pair = [], []
    for n in range(4):
        lanes = []
        for i in range(3):
            pieces = []
            for r in range(8):
                at = 8 * ((n * 3 + i) * 8 + r)
                one = found[at : at + 8]
                both = jnp.where(half_b[n * 3 + i], one, pltpu.roll(one, 64, 1))
                pieces.append(jnp.concatenate([both, both], axis=0).astype(BF) * halves)
            lanes.append(jnp.concatenate(pieces, axis=0))
        pair.append(couple(jnp.concatenate(lanes, axis=1), v_cb[n]))
        if n % 2:
            rows.append(fold_pair(jnp.concatenate(pair, axis=0)))
            pair = []
    near_b = nn(jnp.concatenate(rows, axis=0), expand[:, 0:128])


    own_c = v_tc[pl.ds(pl.multiple_of(64 * y, 64), 64), :]
    own_c = jnp.where(core == 0, own_c[:, 0:256].astype(F32), own_c[:, 256:512].astype(F32)).astype(BF)
    down_c = jnp.concatenate(
        [nn(own_c[:, 64 * b : 64 * b + 64], v_tb[64 * b : 64 * b + 64, :]) for b in range(4)], axis=1
    ).astype(BF)

    received(share_in.at[pl.ds(0, 4)], s_recv.at[1])
    grand_rows = 16 * groups
    row, lane32 = grid_index((32, 128), 0), grid_index((32, 128), 1)
    choose_c, half_c = [], []
    for source in range(8):
        code = jnp.broadcast_to(share_in[source, 0:16, :].astype(F32)[3:4], (32, 128))
        code = jnp.sum(jnp.where(lane32 == row // 8, code, 0.0), axis=1, keepdims=True).astype(jnp.int32)
        row1 = grid_index((32, 1), 0)
        base = jnp.where((code >= 0) & (row1 < 24), (code // 2) * 8 + row1 % 8, -1000)
        hit = jnp.broadcast_to(base, (32, grand_rows)) == grid_index((32, grand_rows), 1)
        choose_c.append(flag(hit))
        half_c.append(jnp.broadcast_to(code % 2, (32, 128)) == lane32 // 64)
    choose_c = jnp.concatenate(choose_c, axis=0).astype(BF)
    half_c = jnp.concatenate(half_c, axis=0)
    blocks_c = jnp.concatenate([share_in[source] for source in range(8)], axis=1)
    row, col = grid_index((64, 128), 0), grid_index((64, 128), 1)
    same_c = row // 16 == col % 4
    row, col = grid_index((256, 64), 0), grid_index((256, 64), 1)
    expand_c = flag(col == 2 * ((row % 128) // 4) + row // 128).astype(BF)

    for k in range(4):
        if k == 0:
            block = leaf_window.at[8 + (1 - core) * 4 + y]
        else:
            block = leaf_window.at[8 + (1 - core) * 4 + lax.rem(y + 4 - k, 4)]
        received(block, mate_recv.at[k])
    for d in range(4):
        source = (1 - core) * 4 + lax.rem(y + 4 - d, 4)
        for side in range(2):
            received(
                leaf_window.at[source + 16 * side], mate_recv.at[4 + 2 * d + side], (has_down, has_up)[side]
            )
    loads[6].wait()
    for half in range(2):
        window = jnp.concatenate(
            [
                leaf_window[:, 32 * k : 32 * k + 32, :].reshape(768, 128)
                for k in (2 * half, 2 * half + 1)
            ],
            axis=1,
        )
        picked[:, 256 * half : 256 * half + 256] = nn(pick_a[...], window)

    def build(n, carry):
        lanes = []
        for i in range(3):
            eight = picked[pl.ds(pl.multiple_of(24 * n + 8 * i, 8), 8), :]
            pieces = []
            for k in range(4):
                one = eight[:, 128 * k : 128 * k + 128]
                turned = pltpu.roll(one, 64, 1)
                pieces.append(jnp.concatenate([one, turned], axis=0).astype(BF) * halves)
                pieces.append(jnp.concatenate([turned, one], axis=0).astype(BF) * halves)
            lanes.append(jnp.concatenate(pieces, axis=0))
        left_side[n] = jnp.concatenate(lanes, axis=1)
        return carry

    def multiply(n, carry):
        products[n] = couple(left_side[n], v_ca.at[n])
        return carry

    def fold_products(pair, carry):
        rows = products[pl.ds(2 * pair, 2)].reshape(256, 256)
        folded[pl.ds(pl.multiple_of(16 * pair, 16), 16), :] = fold_pair(rows)
        return carry

    lax.fori_loop(0, 32, build, 0, unroll=32)
    lax.fori_loop(0, 32, multiply, 0, unroll=32)
    lax.fori_loop(0, 16, fold_products, 0, unroll=16)
    near_a = nn(folded[...], expand)
    for h in range(2):
        y_b = jnp.where(diagonal2[0:16], near_b[16 * h : 16 * h + 16], 0.0).astype(BF)
        spread_b = nn(y_b, v_tb[128 * h : 128 * h + 128, :])
        for j in range(2):
            for k in range(2):
                s = 4 * h + 2 * j + k
                part = spread_b[8 * j : 8 * j + 8, 256 * k : 256 * k + 256]
                near[32 * s : 32 * s + 32, :] = near_a[32 * s : 32 * s + 32] + jnp.concatenate([part] * 4, axis=0)

    received(grand_window.at[pl.ds(0, groups - 1)], c_recv.at[0])
    found = nn(choose_c, grand_window[...].reshape(grand_rows, 128))
    found = jnp.where(half_c, found, pltpu.roll(found, 64, 1))
    lanes = []
    for source in range(8):
        pieces = []
        for e in range(4):
            one = found[32 * source + 8 * e : 32 * source + 8 * e + 8]
            pieces.append(jnp.concatenate([one, one], axis=0).astype(BF) * halves)
        lanes.append(jnp.concatenate(pieces, axis=0))
    full = jnp.where(same_c, nt(jnp.concatenate(lanes, axis=1), blocks_c), 0.0)
    full = full[0:16] + full[16:32] + full[32:48] + full[48:64]
    y_c = nn(jnp.concatenate([full[0:8], full[8:16]], axis=1).astype(BF), expand_c).astype(BF)

    from_c = nn(y_c, down_c)
    writes = []
    for s in range(8):
        part = from_c[:, 256 * s : 256 * s + 256]
        part = near[32 * s : 32 * s + 32, :] + jnp.concatenate([part] * 4, axis=0)
        y_a = jnp.where(diagonal4, part, 0.0).astype(BF)
        rows = pl.ds(32 * s, 32)
        field[rows, :] = nn(y_a, v_basis[256 * s : 256 * s + 256, :]).astype(BF)
        writes.append(pltpu.make_async_copy(field.at[rows], out.at[rows], out_sem.at[s]))
        writes[-1].start()

    for copy, when in sent:
        pl.when(when)(copy.wait_send)
    for write in writes:
        write.wait()


def tiles(coupling):
    boxes = coupling.shape[0]
    split = coupling.reshape(boxes, 3, 8, 32, 128)
    return split.transpose(0, 1, 3, 2, 4).reshape(boxes, 768, 128)


def on_device(
    values,
    basis,
    transfer_b,
    transfer_c,
    coupling_a,
    lists_a,
    mask_a,
    coupling_b,
    lists_b,
    mask_b,
    coupling_c,
    lists_c,
    mask_c,
):
    groups = lax.axis_size("leaf")
    operands = (
        values.reshape(256, 256),
        basis.reshape(2048, 256),
        transfer_b.reshape(256, 512),
        transfer_c.reshape(256, 512),
        tiles(coupling_a[0]),
        tiles(coupling_b[0]),
        coupling_c[0].transpose(1, 0, 2),
        lists_a[0].T,
        mask_a[0].T,
        lists_b[0],
        mask_b[0],
        lists_c.transpose(2, 0, 1),
        mask_c.transpose(2, 0, 1),
    )
    far = pl.BlockSpec(memory_space=pltpu.HBM)
    dma = pltpu.SemaphoreType.DMA
    field = pl.pallas_call(
        functools.partial(kernel, groups),
        out_shape=jax.ShapeDtypeStruct((256, 256), BF),
        in_specs=[far] * 13,
        out_specs=far,
        scratch_shapes=[pltpu.VMEM(x.shape, x.dtype) for x in operands]
        + [
            pltpu.VMEM((24, 128, 128), BF),
            pltpu.VMEM((24, 16, 128), BF),
            pltpu.VMEM((groups, 16, 128), BF),
            pltpu.VMEM((4, 128, 128), BF),
            pltpu.VMEM((8, 128, 128), BF),
            pltpu.VMEM((768, 768), BF),
            pltpu.VMEM((768, 512), F32),
            pltpu.VMEM((32, 128, 384), BF),
            pltpu.VMEM((32, 128, 256), BF),
            pltpu.VMEM((256, 512), BF),
            pltpu.VMEM((256, 256), F32),
            pltpu.VMEM((256, 256), BF),
            dma((8,)),
        ]
        + [dma((k,)) for k in (13, 3, 3, 8, 8, 12, 12, 7, 1, 2, 2, groups - 1, 1)]
        + [pltpu.SemaphoreType.REGULAR((3,)), dma((4,)), dma((2,))],
        compiler_params=pltpu.CompilerParams(
            collective_id=0, has_side_effects=True, vmem_limit_bytes=60 * 1024 * 1024
        ),
        cost_estimate=pl.CostEstimate(flops=5_000_000_000, bytes_accessed=10_000_000, transcendentals=0),
        name="far_field",
    )(*operands)
    return field.reshape(1, 32, 8, 256)


def solution(mesh):
    in_specs = (
        P("leaf", "tel", None, None),
        P("leaf", "tel", None, None),
        P("leaf", "tel", None, None),
        P("leaf", None, None, None),
        P("leaf", "tel", None, None),
        P("leaf", "tel", None),
        P("leaf", "tel", None),
        P("leaf", "tel", None, None),
        P("leaf", "tel", None),
        P("leaf", "tel", None),
        P("leaf", None, "tel", None),
        P("leaf", None, "tel"),
        P("leaf", None, "tel"),
    )
    out_specs = P("leaf", "tel", None, None)
    return jax.shard_map(
        on_device, mesh=mesh, in_specs=in_specs, out_specs=out_specs, check_vma=False
    )
```

```python
import functools

import jax
import jax.numpy as jnp
from jax import lax
from jax.experimental import pallas as pl
from jax.experimental.pallas import tpu as pltpu
from jax.sharding import PartitionSpec as P

BF = jnp.bfloat16
F32 = jnp.float32
MESH = pl.DeviceIdType.MESH


def nt(a, b):
    return lax.dot_general(a, b, (((1,), (1,)), ((), ())), preferred_element_type=F32)


def nn(a, b):
    return jnp.dot(a, b, preferred_element_type=F32)


def grid_index(shape, dim):
    return lax.broadcasted_iota(jnp.int32, shape, dim)


def flag(condition):
    return jnp.where(condition, 1.0, 0.0)


def far_first(depth):
    offsets = [(dz, dx) for dz in range(depth) for dx in range(4) if dz or dx]
    return sorted(offsets, key=lambda o: -(min(o[0], depth - o[0]) + min(o[1], 4 - o[1])))


def column(rows, height, stride):
    sub, lane = grid_index((height, 128), 0), grid_index((height, 128), 1)
    total = jnp.zeros((height, 128), F32)
    for place, row in enumerate(rows):
        width = row.shape[1]
        wide = jnp.concatenate([row.astype(F32), jnp.zeros((1, 128 - width), F32)], axis=1)
        hit = (lane == sub - place * stride) & (lane < width)
        total = total + jnp.where(hit, jnp.broadcast_to(wide, (height, 128)), 0.0)
    return jnp.sum(total, axis=1, keepdims=True).astype(jnp.int32)


def kernel(
    groups,
    values,
    basis,
    transfer_b,
    transfer_c,
    coupling_a,
    coupling_b,
    coupling_c,
    lists_a,
    mask_a,
    lists_b,
    mask_b,
    lists_c,
    mask_c,
    out,
    v_values,
    v_basis,
    v_tb,
    v_tc,
    v_ca,
    v_cb,
    v_cc,
    v_lists_a,
    v_mask_a,
    v_lists_b,
    v_mask_b,
    v_lists_c,
    v_mask_c,
    leaf_window,
    parent_window,
    grand_window,
    share_out,
    share_in,
    pick_a,
    picked,
    left_side,
    products,
    folded,
    near,
    field,
    out_sem,
    load_sem,
    y_send,
    y_recv,
    x_send,
    x_recv,
    mate_send,
    mate_recv,
    b_send,
    b_recv,
    bx_send,
    bx_recv,
    c_send,
    c_recv,
    here,
    s_send,
    s_recv,
):
    g = lax.axis_index("leaf")
    t = lax.axis_index("tel")
    y, core = t // 2, t % 2
    depth = groups // 4

    def group_at(dz, dx):
        return lax.rem(g // 4 + dz, depth) * 4 + lax.rem(g + dx, 4)

    up, down = lax.rem(g + 1, groups), lax.rem(g + groups - 1, groups)

    loads = [
        pltpu.make_async_copy(source, target, load_sem.at[place])
        for place, (source, target) in enumerate(
            (
                (values, v_values),
                (basis, v_basis),
                (transfer_b, v_tb),
                (transfer_c, v_tc),
                (coupling_c, v_cc),
                (coupling_b, v_cb),
                (coupling_a, v_ca),
                (lists_a, v_lists_a),
                (mask_a, v_mask_a),
                (lists_b, v_lists_b),
                (mask_b, v_mask_b),
                (lists_c, v_lists_c),
                (mask_c, v_mask_c),
            )
        )
    ]
    for load in loads[0:3]:
        load.start()

    barrier = pltpu.get_barrier_semaphore()

    def greet_group(d, carry):
        pl.semaphore_signal(
            barrier, inc=1, device_id={"tel": lax.rem(t + d, 8), "leaf": g}, device_id_type=MESH
        )
        return carry

    lax.fori_loop(1, 8, greet_group, 0)
    half = groups // 2
    z, upper_half = g // 4, g >= half
    lower_half = jnp.logical_not(upper_half)

    def signal(semaphore, target):
        pl.semaphore_signal(
            semaphore, inc=1, device_id={"tel": t, "leaf": target}, device_id_type=MESH
        )

    def signal_plane(offset, along_x, when):
        @pl.when(when)
        def _():
            for dx in along_x:
                signal(barrier, (z + offset) * 4 + lax.rem(g + dx, 4))

    def signal_half(semaphore, start, when):
        def one(d, carry):
            signal(semaphore, start + lax.rem(g + d, half))
            return carry

        @pl.when(when)
        def _():
            lax.fori_loop(0, half, one, 0)

    signal_half(barrier, half, lower_half)
    signal_plane(0, (1, 2, 3), True)
    signal_plane(1, range(4), upper_half & (z < depth - 1))
    signal_plane(-1, range(4), z > depth // 2)
    first_x, last_x = g % 4 == 0, g % 4 == 3
    pl.when(lower_half & last_x & (z < depth // 2 - 1))(lambda: signal(barrier, g + 1))
    pl.when(first_x & (z > 0) & (z <= depth // 2))(lambda: signal(barrier, g - 1))

    sub, lane = grid_index((8, 128), 0), grid_index((8, 128), 1)
    left = lane < 64
    even_left = (sub % 2 == 0) & left
    odd_right = (sub % 2 == 1) & (lane >= 64)

    for end, first in ((0, 0), (groups - 1, 16)):

        @pl.when(g == end)
        def _():
            leaf_window[first : first + 8] = jnp.zeros((8, 128, 128), BF)
            parent_window[first : first + 8] = jnp.zeros((8, 16, 128), BF)

    beside = (z > depth // 2).astype(jnp.int32) + (z < depth - 1).astype(jnp.int32)
    pl.when(upper_half)(lambda: pl.semaphore_wait(barrier, 10 + 4 * beside + half))
    signal_half(here.at[0], 0, upper_half)
    pl.when(upper_half & (z < depth - 1))(lambda: signal(here.at[1], g + 4))
    pl.when(upper_half & (z > depth // 2))(lambda: signal(here.at[1], g - 4))
    loads[0].wait()
    loads[1].wait()
    for load in loads[7:13] + loads[3:7]:
        load.start()
    placed, stacked = [], []
    for s in range(8):
        product = nt(v_values[32 * s : 32 * s + 32, :], v_basis[256 * s : 256 * s + 256, :])
        for h in range(2):
            first = product[16 * h : 16 * h + 8, 128 * h : 128 * h + 128]
            second = product[16 * h + 8 : 16 * h + 16, 128 * h : 128 * h + 128]
            placed.append(
                jnp.where(even_left, first, jnp.where(odd_right, pltpu.roll(first, 64, 1), 0.0))
            )
            placed.append(
                jnp.where(even_left, pltpu.roll(second, 64, 1), jnp.where(odd_right, second, 0.0))
            )
            stacked.append(jnp.where(left, first, second))
    placed = jnp.concatenate(placed, axis=0).astype(BF)
    row = grid_index((128, 1), 0)
    first = (row % 32) * 8 + (row // 32) * 2
    order = flag(jnp.broadcast_to(first, (128, 256)) == (grid_index((128, 256), 1) & -2)).astype(BF)
    own_slot = 8 + core * 4 + y
    leaf_window[own_slot] = nn(order, placed).astype(BF)

    loads[2].wait()
    lifted = []
    for b in range(4):
        children = jnp.concatenate(stacked[4 * b : 4 * b + 4], axis=1).astype(BF)
        lifted.append(nt(children, v_tb[64 * b : 64 * b + 64, :]))
    parent_window[8 + t] = jnp.concatenate(
        [jnp.concatenate(lifted[0:2], axis=1), jnp.concatenate(lifted[2:4], axis=1)], axis=0
    ).astype(BF)

    def send(source, target, send_sem, recv_sem, tel, leaf, when=True):
        copy = pltpu.make_async_remote_copy(
            src_ref=source,
            dst_ref=target,
            send_sem=send_sem,
            recv_sem=recv_sem,
            device_id={"tel": tel, "leaf": leaf},
            device_id_type=MESH,
        )
        pl.when(when)(copy.start)
        return copy, when

    ends = last_x.astype(jnp.int32) + (first_x & (z > 0)).astype(jnp.int32)
    pl.when(lower_half)(lambda: pl.semaphore_wait(barrier, 10 + ends))

    sent = []
    for d in range(1, 8):
        block = parent_window.at[8 + t]
        sent.append(send(block, block, b_send.at[d - 1], b_recv.at[0], lax.rem(t + d, 8), g))

    mate = t + 1 - 2 * core

    has_up, has_down = g < groups - 1, g > 0

    def spread(slot, place):
        block = leaf_window.at[slot]
        sent.append(
            send(block, leaf_window.at[slot - 8], x_send.at[place], x_recv.at[place], t, up, has_up)
        )
        sent.append(
            send(
                block, leaf_window.at[slot + 8], x_send.at[4 + place], x_recv.at[4 + place], t, down, has_down
            )
        )
        sent.append(send(block, block, mate_send.at[place], mate_recv.at[place], mate, g))

    own = leaf_window.at[own_slot]
    for d in range(1, 4):
        sent.append(
            send(own, own, y_send.at[d - 1], y_recv.at[d - 1], lax.rem(y + d, 4) * 2 + core, g)
        )
    spread(own_slot, 0)

    @pl.when(upper_half)
    def _():
        pl.semaphore_wait(here.at[1], 1 + ((z > depth // 2) & (z < depth - 1)).astype(jnp.int32))
        signal(here.at[2], jnp.where(z < depth // 2 + 2, g + 8, g - 8))

    def received(ref, sem, when=True):
        pl.when(when)(pltpu.make_async_copy(ref, ref, sem).wait)

    loads[7].wait()
    loads[8].wait()
    local = v_lists_a[...] - (g - 1) * 256
    inner = local % 256
    slot = (local // 256) * 8 + ((inner // 32) % 2) * 4 + inner // 64
    place = jnp.where(v_mask_a[...] == 1, slot * 32 + inner % 32, -1)
    lane24 = grid_index((24, 128), 1)
    for pair in range(16):
        rows = []
        for n in (2 * pair, 2 * pair + 1):
            wide = jnp.broadcast_to(place[:, n : n + 1], (24, 128)) - lane24
            rows.append(jnp.concatenate([flag(wide == 128 * k) for k in range(6)], axis=1))
        pick_a[48 * pair : 48 * pair + 48, :] = jnp.concatenate(rows, axis=0).astype(BF)

    for d in range(1, 4):
        source = 8 + core * 4 + lax.rem(y + 4 - d, 4)
        received(leaf_window.at[source], y_recv.at[d - 1])
        spread(source, d)

    received(parent_window.at[pl.ds(0, 7)], b_recv.at[0])
    loads[3].wait()
    lifted = []
    for c in range(4):
        one = parent_window[8 + 2 * c].astype(F32)
        two = parent_window[9 + 2 * c].astype(F32)
        children = jnp.concatenate([one[0:8], one[8:16], two[0:8], two[8:16]], axis=1).astype(BF)
        lifted.append(nt(children, v_tc[64 * c : 64 * c + 64, :]))
    grand_window[g] = jnp.concatenate(
        [jnp.concatenate(lifted[0:2], axis=1), jnp.concatenate(lifted[2:4], axis=1)], axis=0
    ).astype(BF)

    block = grand_window.at[g]
    grand_copies = [
        pltpu.make_async_remote_copy(
            src_ref=block,
            dst_ref=block,
            send_sem=c_send.at[k],
            recv_sem=c_recv.at[0],
            device_id={"tel": t, "leaf": group_at(dz, dx)},
            device_id_type=MESH,
        )
        for k, (dz, dx) in enumerate(far_first(depth))
    ]
    sent.extend((copy, True) for copy in grand_copies)

    def send_grand(semaphore, count):
        pl.semaphore_wait(semaphore, count)
        for copy in grand_copies:
            copy.start()

    pl.when(upper_half)(lambda: send_grand(here.at[2], 1))

    loads[4].wait()
    for load in loads[9:13]:
        load.wait()
    codes = jnp.zeros((4, 128), F32)
    lane4 = grid_index((4, 128), 1)
    for p in range(3):
        entry = column([v_lists_c[p]], 4, 0)
        valid = column([v_mask_c[p]], 4, 0)
        code = jnp.where(valid == 1, entry, -1).astype(F32)
        codes = jnp.where(lane4 == p, jnp.broadcast_to(code, (4, 128)), codes)
    codes = jnp.concatenate([codes, jnp.zeros((4, 4096 - 128), F32)], axis=1)
    upper = jnp.concatenate([v_cc[0].astype(F32), v_cc[1].astype(F32)], axis=0)
    lower = jnp.concatenate([v_cc[2].astype(F32), codes], axis=0)
    blocks_c = []
    for k in range(32):
        blocks_c.append(upper[:, 128 * k : 128 * k + 128])
        blocks_c.append(lower[:, 128 * k : 128 * k + 128])
    blocks_c = jnp.concatenate(blocks_c, axis=0).astype(BF)
    row = grid_index((512, 1), 0)
    source = ((row % 128) // 4) * 16 + (row % 4) * 4 + row // 128
    regroup = flag(jnp.broadcast_to(source, (512, 512)) == grid_index((512, 512), 1))
    blocks_c = nn(regroup.astype(BF), blocks_c).astype(BF)
    for c in range(4):
        share_out[c] = blocks_c[128 * c : 128 * c + 128]
    share_in[core * 4 + y] = share_out[y]
    for d in range(1, 4):
        owner = lax.rem(y + d, 4)
        sent.append(
            send(
                share_out.at[owner],
                share_in.at[core * 4 + y],
                s_send.at[d - 1],
                s_recv.at[0],
                owner * 2 + core,
                g,
            )
        )

    choose_b, half_b = [], []
    lane384 = grid_index((8, 384), 1)
    for n in range(4):
        entry = column([v_lists_b[n : n + 1, :]], 24, 0) - (g - 1) * 32
        valid = column([v_mask_b[n : n + 1, :]], 24, 0)
        base = jnp.where(valid == 1, (entry // 2) * 8, -1000)
        for i in range(3):
            wide = jnp.broadcast_to(base[8 * i : 8 * i + 8], (8, 384)) - lane384
            choose_b.extend(flag(wide == -r) for r in range(8))
            half_b.append(jnp.broadcast_to(entry[8 * i : 8 * i + 8] % 2, (8, 128)) == lane // 64)
    choose_b = jnp.concatenate(choose_b, axis=0).astype(BF)

    group_parents = parent_window.at[pl.ds(8, 8)]
    sent.append(
        send(group_parents, parent_window.at[pl.ds(0, 8)], bx_send.at[0], bx_recv.at[0], t, up, has_up)
    )
    sent.append(
        send(group_parents, parent_window.at[pl.ds(16, 8)], bx_send.at[1], bx_recv.at[1], t, down, has_down)
    )

    late = lower_half & last_x & (z == depth // 2 - 1)
    pl.when(late)(lambda: send_grand(here.at[0], half))
    received(share_in.at[pl.ds(0, 3)], s_recv.at[0])
    shares = share_in.at[pl.ds(core * 4, 4)]
    sent.append(send(shares, shares, s_send.at[3], s_recv.at[1], mate, g))

    for d in range(4):
        source = core * 4 + lax.rem(y + 4 - d, 4)
        for side in range(2):
            block = leaf_window.at[source + 16 * side]
            there = (has_down, has_up)[side]
            received(block, x_recv.at[4 * side + d], there)
            k = 4 + 2 * d + side
            sent.append(send(block, block, mate_send.at[k], mate_recv.at[k], mate, g, there))


    row, col = grid_index((128, 256), 0), grid_index((128, 256), 1)
    same_p = row % 8 == col % 8
    row, col = grid_index((32, 256), 0), grid_index((32, 256), 1)
    fold = flag(
        ((row // 8) % 2 == col // 128) & (row % 8 == (col // 16) % 8) & (row // 16 == (col // 8) % 2)
    ).astype(BF)
    diagonal4 = row // 8 == col // 64
    row = grid_index((512, 1), 0)
    target = 2 * ((row % 256) // 8) + row // 256
    expand = flag(jnp.broadcast_to(target, (512, 128)) == grid_index((512, 128), 1) % 64).astype(BF)
    expand = jnp.concatenate([expand, expand], axis=1)
    row, col = grid_index((32, 128), 0), grid_index((32, 128), 1)
    diagonal2 = (row // 8) % 2 == col // 64
    row, col = grid_index((16, 128), 0), grid_index((16, 128), 1)
    halves = flag(row // 8 == col // 64).astype(BF)

    def couple(lhs, coupling):
        wide = jnp.concatenate([coupling[256 * i : 256 * i + 256] for i in range(3)], axis=1)
        return jnp.where(same_p, nt(lhs, wide), 0.0).astype(BF)

    def fold_pair(pair):
        both = nn(fold, pair)
        return jnp.concatenate([both[0:16], both[16:32]], axis=1).astype(BF)

    pl.when(lower_half & jnp.logical_not(late))(lambda: send_grand(here.at[0], half))

    received(parent_window.at[pl.ds(0, 8)], bx_recv.at[0], has_down)
    received(parent_window.at[pl.ds(16, 8)], bx_recv.at[1], has_up)
    loads[5].wait()
    found = nn(choose_b, parent_window[...].reshape(384, 128))
    rows, pair = [], []
    for n in range(4):
        lanes = []
        for i in range(3):
            pieces = []
            for r in range(8):
                at = 8 * ((n * 3 + i) * 8 + r)
                one = found[at : at + 8]
                both = jnp.where(half_b[n * 3 + i], one, pltpu.roll(one, 64, 1))
                pieces.append(jnp.concatenate([both, both], axis=0).astype(BF) * halves)
            lanes.append(jnp.concatenate(pieces, axis=0))
        pair.append(couple(jnp.concatenate(lanes, axis=1), v_cb[n]))
        if n % 2:
            rows.append(fold_pair(jnp.concatenate(pair, axis=0)))
            pair = []
    near_b = nn(jnp.concatenate(rows, axis=0), expand[:, 0:128])


    own_c = v_tc[pl.ds(pl.multiple_of(64 * y, 64), 64), :]
    own_c = jnp.where(core == 0, own_c[:, 0:256].astype(F32), own_c[:, 256:512].astype(F32)).astype(BF)
    down_c = jnp.concatenate(
        [nn(own_c[:, 64 * b : 64 * b + 64], v_tb[64 * b : 64 * b + 64, :]) for b in range(4)], axis=1
    ).astype(BF)

    received(share_in.at[pl.ds(0, 4)], s_recv.at[1])
    grand_rows = 16 * groups
    row, lane32 = grid_index((32, 128), 0), grid_index((32, 128), 1)
    choose_c, half_c = [], []
    for source in range(8):
        code = jnp.broadcast_to(share_in[source, 0:16, :].astype(F32)[3:4], (32, 128))
        code = jnp.sum(jnp.where(lane32 == row // 8, code, 0.0), axis=1, keepdims=True).astype(jnp.int32)
        row1 = grid_index((32, 1), 0)
        base = jnp.where((code >= 0) & (row1 < 24), (code // 2) * 8 + row1 % 8, -1000)
        hit = jnp.broadcast_to(base, (32, grand_rows)) == grid_index((32, grand_rows), 1)
        choose_c.append(flag(hit))
        half_c.append(jnp.broadcast_to(code % 2, (32, 128)) == lane32 // 64)
    choose_c = jnp.concatenate(choose_c, axis=0).astype(BF)
    half_c = jnp.concatenate(half_c, axis=0)
    blocks_c = jnp.concatenate([share_in[source] for source in range(8)], axis=1)
    row, col = grid_index((64, 128), 0), grid_index((64, 128), 1)
    same_c = row // 16 == col % 4
    row, col = grid_index((256, 64), 0), grid_index((256, 64), 1)
    expand_c = flag(col == 2 * ((row % 128) // 4) + row // 128).astype(BF)

    for k in range(4):
        if k == 0:
            block = leaf_window.at[8 + (1 - core) * 4 + y]
        else:
            block = leaf_window.at[8 + (1 - core) * 4 + lax.rem(y + 4 - k, 4)]
        received(block, mate_recv.at[k])
    for d in range(4):
        source = (1 - core) * 4 + lax.rem(y + 4 - d, 4)
        for side in range(2):
            received(
                leaf_window.at[source + 16 * side], mate_recv.at[4 + 2 * d + side], (has_down, has_up)[side]
            )
    loads[6].wait()
    for half in range(2):
        window = jnp.concatenate(
            [
                leaf_window[:, 32 * k : 32 * k + 32, :].reshape(768, 128)
                for k in (2 * half, 2 * half + 1)
            ],
            axis=1,
        )
        picked[:, 256 * half : 256 * half + 256] = nn(pick_a[...], window)

    def build(n, carry):
        lanes = []
        for i in range(3):
            eight = picked[pl.ds(pl.multiple_of(24 * n + 8 * i, 8), 8), :]
            pieces = []
            for k in range(4):
                one = eight[:, 128 * k : 128 * k + 128]
                turned = pltpu.roll(one, 64, 1)
                pieces.append(jnp.concatenate([one, turned], axis=0).astype(BF) * halves)
                pieces.append(jnp.concatenate([turned, one], axis=0).astype(BF) * halves)
            lanes.append(jnp.concatenate(pieces, axis=0))
        left_side[n] = jnp.concatenate(lanes, axis=1)
        return carry

    def multiply(n, carry):
        products[n] = couple(left_side[n], v_ca.at[n])
        return carry

    def fold_products(pair, carry):
        rows = products[pl.ds(2 * pair, 2)].reshape(256, 256)
        folded[pl.ds(pl.multiple_of(16 * pair, 16), 16), :] = fold_pair(rows)
        return carry

    lax.fori_loop(0, 32, build, 0, unroll=32)
    lax.fori_loop(0, 32, multiply, 0, unroll=32)
    lax.fori_loop(0, 16, fold_products, 0, unroll=16)
    near_a = nn(folded[...], expand)
    for h in range(2):
        y_b = jnp.where(diagonal2[0:16], near_b[16 * h : 16 * h + 16], 0.0).astype(BF)
        spread_b = nn(y_b, v_tb[128 * h : 128 * h + 128, :])
        for j in range(2):
            for k in range(2):
                s = 4 * h + 2 * j + k
                part = spread_b[8 * j : 8 * j + 8, 256 * k : 256 * k + 256]
                near[32 * s : 32 * s + 32, :] = near_a[32 * s : 32 * s + 32] + jnp.concatenate([part] * 4, axis=0)

    received(grand_window.at[pl.ds(0, groups - 1)], c_recv.at[0])
    found = nn(choose_c, grand_window[...].reshape(grand_rows, 128))
    found = jnp.where(half_c, found, pltpu.roll(found, 64, 1))
    lanes = []
    for source in range(8):
        pieces = []
        for e in range(4):
            one = found[32 * source + 8 * e : 32 * source + 8 * e + 8]
            pieces.append(jnp.concatenate([one, one], axis=0).astype(BF) * halves)
        lanes.append(jnp.concatenate(pieces, axis=0))
    full = jnp.where(same_c, nt(jnp.concatenate(lanes, axis=1), blocks_c), 0.0)
    full = full[0:16] + full[16:32] + full[32:48] + full[48:64]
    y_c = nn(jnp.concatenate([full[0:8], full[8:16]], axis=1).astype(BF), expand_c).astype(BF)

    from_c = nn(y_c, down_c)
    writes = []
    for s in range(8):
        part = from_c[:, 256 * s : 256 * s + 256]
        part = near[32 * s : 32 * s + 32, :] + jnp.concatenate([part] * 4, axis=0)
        y_a = jnp.where(diagonal4, part, 0.0).astype(BF)
        rows = pl.ds(32 * s, 32)
        field[rows, :] = nn(y_a, v_basis[256 * s : 256 * s + 256, :]).astype(BF)
        writes.append(pltpu.make_async_copy(field.at[rows], out.at[rows], out_sem.at[s]))
        writes[-1].start()

    for copy, when in sent:
        pl.when(when)(copy.wait_send)
    for write in writes:
        write.wait()


def tiles(coupling):
    boxes = coupling.shape[0]
    split = coupling.reshape(boxes, 3, 8, 32, 128)
    return split.transpose(0, 1, 3, 2, 4).reshape(boxes, 768, 128)


def on_device(
    values,
    basis,
    transfer_b,
    transfer_c,
    coupling_a,
    lists_a,
    mask_a,
    coupling_b,
    lists_b,
    mask_b,
    coupling_c,
    lists_c,
    mask_c,
):
    groups = lax.axis_size("leaf")
    operands = (
        values.reshape(256, 256),
        basis.reshape(2048, 256),
        transfer_b.reshape(256, 512),
        transfer_c.reshape(256, 512),
        tiles(coupling_a[0]),
        tiles(coupling_b[0]),
        coupling_c[0].transpose(1, 0, 2),
        lists_a[0].T,
        mask_a[0].T,
        lists_b[0],
        mask_b[0],
        lists_c.transpose(2, 0, 1),
        mask_c.transpose(2, 0, 1),
    )
    far = pl.BlockSpec(memory_space=pltpu.HBM)
    dma = pltpu.SemaphoreType.DMA
    field = pl.pallas_call(
        functools.partial(kernel, groups),
        out_shape=jax.ShapeDtypeStruct((256, 256), BF),
        in_specs=[far] * 13,
        out_specs=far,
        scratch_shapes=[pltpu.VMEM(x.shape, x.dtype) for x in operands]
        + [
            pltpu.VMEM((24, 128, 128), BF),
            pltpu.VMEM((24, 16, 128), BF),
            pltpu.VMEM((groups, 16, 128), BF),
            pltpu.VMEM((4, 128, 128), BF),
            pltpu.VMEM((8, 128, 128), BF),
            pltpu.VMEM((768, 768), BF),
            pltpu.VMEM((768, 512), F32),
            pltpu.VMEM((32, 128, 384), BF),
            pltpu.VMEM((32, 128, 256), BF),
            pltpu.VMEM((256, 512), BF),
            pltpu.VMEM((256, 256), F32),
            pltpu.VMEM((256, 256), BF),
            dma((8,)),
        ]
        + [dma((k,)) for k in (13, 3, 3, 8, 8, 12, 12, 7, 1, 2, 2, groups - 1, 1)]
        + [pltpu.SemaphoreType.REGULAR((3,)), dma((4,)), dma((2,))],
        compiler_params=pltpu.CompilerParams(
            collective_id=0, has_side_effects=True, vmem_limit_bytes=60 * 1024 * 1024
        ),
        cost_estimate=pl.CostEstimate(flops=5_000_000_000, bytes_accessed=10_000_000, transcendentals=0),
        name="far_field",
    )(*operands)
    return field.reshape(1, 32, 8, 256)


def solution(mesh):
    in_specs = (
        P("leaf", "tel", None, None),
        P("leaf", "tel", None, None),
        P("leaf", "tel", None, None),
        P("leaf", None, None, None),
        P("leaf", "tel", None, None),
        P("leaf", "tel", None),
        P("leaf", "tel", None),
        P("leaf", "tel", None, None),
        P("leaf", "tel", None),
        P("leaf", "tel", None),
        P("leaf", None, "tel", None),
        P("leaf", None, "tel"),
        P("leaf", None, "tel"),
    )
    out_specs = P("leaf", "tel", None, None)
    return jax.shard_map(
        on_device, mesh=mesh, in_specs=in_specs, out_specs=out_specs, check_vma=False
    )
```
